32 devices in a mesh: dp: 4 (over y, x), expert: 8 (over z, core).
Axes of the slice: x: 2, y: 2, z: 4, core: 2. Of those that a mesh axis runs over, the one named last changes fastest.
Arguments:
- tokens: bfloat16 [1024, 4096], P('expert', 'dp'), may hold values from -6 to 6
- expert_ids: int32 [1024, 2], P('expert'), may hold values from 0 to 7, all different within a row; in each aligned block of 128 rows (0 to 127, 128 to 255, ...) at most 40 rows name the same one
- route_weights: float32 [1024, 2], P('expert'), may hold values from 0.1 to 1
- w_gate: bfloat16 [14336, 4096], P('expert', 'dp'), may hold values from -0.09375 to 0.09375
- w_up: bfloat16 [14336, 4096], P('expert', 'dp'), may hold values from -0.09375 to 0.09375
- w_down: bfloat16 [14336, 4096], P('expert', 'dp'), may hold values from -0.125 to 0.125
- out_grad: bfloat16 [1024, 4096], P('expert', 'dp'), may hold values from -0.59765625 to 0.59765625
Outputs:
- output: bfloat16 [1024, 4096], P('expert', 'dp')
- grad_gate: bfloat16 [14336, 4096], P('expert', 'dp')
- grad_up: bfloat16 [14336, 4096], P('expert', 'dp')
- grad_down: bfloat16 [14336, 4096], P('expert', 'dp')
The draws below stay inside these ranges and needn't reach their ends.
Inputs may be any that keep to these rules, and one draw needn't show every extreme that they name: `expert_ids`: each token names two different experts. Among the 128 tokens of one index of expert (aligned blocks of 128 rows), no expert is named more than 40 times, a bound that some block reaches.
All inputs are finite; a program needn't handle non-finite values.
Results may differ from the reference program's by a relative error of at most 0.029.
Values may be sent and summed in bfloat16 or wider, within the bound.
No kernel may reach another device: no remote copies, remote signals or barrier semaphores. Data moves between devices by JAX's collectives and lax.ppermute only.
A program may use at most 128 MiB of HBM per device.

```python
import math
import jax
import jax.numpy as jnp
import numpy as np
from jax import lax

D = 4096
FF = 14336
SLICES = 8
TOK_DEV = 128
H = 1792
EXPERTS = 8
COPIES = 1
FEAT_BLOCKS = 4
CAP = 40
ROWS = 320
TOKENS = 1024


def block_levels(stream_key, shape, split, smallest, top_value):
    def one(dim, blocks):
        heights = jax.random.uniform(jax.random.fold_in(jax.random.fold_in(stream_key, 6), dim), (blocks,), jnp.float32, smallest / len(split), top_value / len(split))
        return jnp.repeat(jnp.exp(heights), shape[dim] // blocks).reshape((-1,) + (1,) * (len(shape) - dim - 1))

    gain = one(*split[0])
    for cut in split[1:]:
        gain = gain * one(*cut)
    return gain


def assign_block(rng, own, number, rows, number_of, top, reach, slope):
    sequence = jax.random.permutation(rng, number_of)
    heavy_load, ordinary = load_shares(number_of, rows * top, reach, slope, True), load_shares(number_of, rows * top, reach, slope, False)
    places = jnp.arange(number_of)

    def named(sizes, offset_by):
        used = int((sizes > 0).sum())
        fixed = max(1, used // 4)
        moved = fixed + (places - fixed + offset_by * (used - fixed)) % max(1, number_of - fixed)
        return jnp.zeros((number_of,), jnp.int32).at[sequence[jnp.where(places < fixed, places, moved)]].set(jnp.asarray(sizes, jnp.int32))

    sizes = jnp.where(number % 4 == 0, named(heavy_load, number // 4), named(ordinary, number - number // 4 - 1))
    mixed = jax.random.permutation(jax.random.fold_in(own, 3), number_of)
    source_of, sink = mixed[0:number_of // 2 * 2:2], mixed[1:number_of // 2 * 2:2]
    room = jnp.minimum(sizes[source_of] - 1, reach - sizes[sink]) // 2
    room = jnp.where((source_of == sequence[0]) | (sink == sequence[0]) | (sizes[sink] == 0), 0, jnp.maximum(room, 0))
    moved = jax.random.randint(jax.random.fold_in(own, 4), (number_of // 2,), 0, 1 << 20) % (room + 1)
    sizes = sizes.at[source_of].add(-moved).at[sink].add(moved)
    labels = jnp.searchsorted(jnp.cumsum(sizes), jnp.arange(rows * top), side="right").astype(jnp.int32)
    table = labels.reshape(top, rows).T
    table = table[jax.random.permutation(jax.random.fold_in(own, 1), rows)]
    offset_by = jax.random.randint(jax.random.fold_in(own, 2), (rows, 1), 0, top)
    return jnp.take_along_axis(table, (jnp.arange(top)[None, :] + offset_by) % top, axis=1)


def load_shares(count, total, limit, lean, full):
    loads = [(1 << 20) // math.isqrt(standing ** lean) + 1 for standing in range(1, count + 1)]
    largest = limit if full else min(limit, max(-(-total // count), total * loads[0] // sum(loads)))
    least = 1 if total - largest >= count - 1 else 0
    given, spare = [largest] + [least] * (count - 1), total - largest - least * (count - 1)
    while spare > 0:
        free = [i for i in range(1, count) if given[i] < largest] or [i for i in range(1, count) if given[i] < limit]
        whole, left = sum([loads[i] for i in free]), spare
        for i in free:
            addition = min(limit - given[i], max(1, left * loads[i] // whole), spare)
            given[i] = given[i] + addition
            spare = spare - addition
    return np.array(given)


def noise(own_key, shape, spread, limit, pieces=(), held_as=jnp.bfloat16):
    level = block_levels(own_key, shape, pieces, -0.22, 0.18) if pieces else 1.0
    drawn = jax.random.normal(own_key, shape, jnp.float32) * spread * level
    return jnp.minimum(jnp.maximum(drawn, -limit), limit).astype(held_as)


def setup_inputs(seed: int = 0) -> dict:
    key_list = jax.random.split(jax.random.key(seed), 8)
    tokens = noise(key_list[0], (TOKENS, D), 1.0, 6.0, ((0, 8), (1, 4)))
    expert_ids_keys = jax.random.split(jax.random.fold_in(key_list[1], 1), TOKENS // TOK_DEV)
    expert_ids_turns = jax.random.permutation(jax.random.fold_in(key_list[1], 3), TOKENS // TOK_DEV)
    expert_ids = jax.vmap(lambda own, number: assign_block(jax.random.fold_in(key_list[1], 2), own, number, TOK_DEV, EXPERTS, 2, CAP, 2))(expert_ids_keys, expert_ids_turns).reshape((TOKENS, 2))
    route_weights = jnp.clip(0.1 + 0.9 * jax.random.uniform(key_list[2], (TOKENS, 2), jnp.float32) ** block_levels(key_list[2], (TOKENS, 2), ((0, 8),), -0.2, 0.2), 0.1, 1.0)
    w_gate = noise(key_list[3], (FF, D), D ** -0.5, 0.09375, ((0, 8), (1, 4)))
    w_up = noise(key_list[4], (FF, D), D ** -0.5, 0.09375, ((0, 8), (1, 4)))
    w_down = noise(key_list[5], (FF, D), H ** -0.5, 0.125, ((0, 8), (1, 4)))
    out_grad = noise(key_list[6], (TOKENS, D), 0.1, 0.59765625, ((0, 8), (1, 4)))
    return dict(tokens=tokens, expert_ids=expert_ids, route_weights=route_weights, w_gate=w_gate, w_up=w_up, w_down=w_down, out_grad=out_grad)


def silu_parts(gate_sum):
    gate_sigmoid = jax.nn.sigmoid(gate_sum)
    return gate_sum * gate_sigmoid, gate_sigmoid * (1.0 + gate_sum * (1.0 - gate_sigmoid))


def blocked(left_rows, right_mat, blocks):
    row_count = left_rows.shape[0]
    feat_count = left_rows.shape[1]
    left_blocks = left_rows.astype(jnp.float32).reshape(row_count, blocks, feat_count // blocks)
    right_blocks = right_mat.astype(jnp.float32).reshape(blocks, feat_count // blocks, right_mat.shape[1])
    partials = jnp.einsum("rqd,qdh->qrh", left_blocks, right_blocks)
    rounded = lax.optimization_barrier(partials.astype(jnp.bfloat16))
    return jnp.sum(rounded.astype(jnp.float32), axis=0)


def tree_sum(stacked):
    while stacked.shape[0] > 1:
        stacked = (stacked[0::2].astype(jnp.float32) + stacked[1::2].astype(jnp.float32)).astype(jnp.bfloat16)
    return stacked[0]


def one_expert(expert, gate_w, up_w, down_w, tokens, flat_ids, flat_weights, out_grad):
    chosen = flat_ids == expert
    picked_rows = jnp.nonzero(chosen, size=ROWS, fill_value=0)[0].astype(jnp.int32)
    is_live = jnp.arange(ROWS, dtype=jnp.int32) < jnp.sum(chosen.astype(jnp.int32))
    tok_index = picked_rows // 2
    gathered = jnp.where(is_live[:, None], tokens[tok_index], jnp.zeros((), jnp.bfloat16))
    gate_sum = blocked(gathered, gate_w.T, FEAT_BLOCKS)
    up_sum = blocked(gathered, up_w.T, FEAT_BLOCKS)
    active, slope_term = silu_parts(gate_sum)
    hidden = (active * up_sum).astype(jnp.bfloat16)
    expert_rows = jnp.dot(hidden, down_w, preferred_element_type=jnp.float32).astype(jnp.bfloat16)
    scale_rows = jnp.where(is_live, flat_weights[picked_rows], jnp.zeros((), jnp.float32))
    cot_rows = (scale_rows[:, None] * out_grad[tok_index].astype(jnp.float32)).astype(jnp.bfloat16)
    grad_hidden = blocked(cot_rows, down_w.T, FEAT_BLOCKS)
    grad_gate_rows = (grad_hidden * up_sum * slope_term).astype(jnp.bfloat16)
    grad_up_rows = (grad_hidden * active).astype(jnp.bfloat16)
    gate_term = jnp.dot(grad_gate_rows.T, gathered, preferred_element_type=jnp.float32).astype(jnp.bfloat16)
    up_term = jnp.dot(grad_up_rows.T, gathered, preferred_element_type=jnp.float32).astype(jnp.bfloat16)
    down_term = jnp.dot(hidden.T, cot_rows, preferred_element_type=jnp.float32).astype(jnp.bfloat16)
    return expert_rows, picked_rows, is_live, gate_term, up_term, down_term


def reference(tokens, expert_ids, route_weights, w_gate, w_up, w_down, out_grad):
    flat_ids = expert_ids.reshape(-1)
    flat_weights = route_weights.reshape(-1)

    def per_slice(slice_index):
        offset = (slice_index * H).astype(jnp.int32)
        gate_w = lax.dynamic_slice_in_dim(w_gate, offset, H, 0)
        up_w = lax.dynamic_slice_in_dim(w_up, offset, H, 0)
        down_w = lax.dynamic_slice_in_dim(w_down, offset, H, 0)

        def per_copy(copy_index):
            return one_expert(slice_index * COPIES + copy_index, gate_w, up_w, down_w, tokens, flat_ids, flat_weights, out_grad)

        rows_out, picked_all, live_all, gate_terms, up_terms, down_terms = lax.map(per_copy, jnp.arange(COPIES, dtype=jnp.int32))
        return rows_out, picked_all, live_all, tree_sum(gate_terms), tree_sum(up_terms), tree_sum(down_terms)

    results = lax.map(per_slice, jnp.arange(SLICES, dtype=jnp.int32))
    expert_rows = results[0].reshape(EXPERTS * ROWS, D)
    targets = jnp.where(results[2].reshape(-1), results[1].reshape(-1), 2 * TOKENS).astype(jnp.int32)
    assigned = jnp.zeros((2 * TOKENS, D), jnp.bfloat16).at[targets].set(expert_rows, mode="drop")
    combined = jnp.sum(route_weights[:, :, None] * assigned.reshape(TOKENS, 2, D).astype(jnp.float32), axis=1)
    output = combined.astype(jnp.bfloat16)
    grad_gate = results[3].reshape(FF, D)
    grad_up = results[4].reshape(FF, D)
    grad_down = results[5].reshape(FF, D)
    return (output, grad_gate, grad_up, grad_down)
```

```python
import jax
import jax.numpy as jnp
from jax import lax
from jax.sharding import PartitionSpec as P

BF = jnp.bfloat16
F32 = jnp.float32


def as_sent(array):

    def short(part):
        return part.astype(BF) if part.dtype == F32 else part

    return jax.tree.map(short, array)


def from_partner(block, axis, bit):
    count = lax.axis_size(axis)
    route = []
    for low in range(count):
        high = low | 1 << bit
        if high != low and high < count:
            route += [(low, high), (high, low)]
    return lax.ppermute(block, axis, route)


def swap(block, axis, mask):
    count = lax.axis_size(axis)
    return lax.ppermute(block, axis, [(i, i ^ mask) for i in range(count)])


def after(value, *earlier):
    return lax.optimization_barrier((value, earlier))[0]


def silu_parts(gate_sum):
    gate_sigmoid = jax.nn.sigmoid(gate_sum)
    return (gate_sum * gate_sigmoid, gate_sigmoid * (1.0 + gate_sum * (1.0 - gate_sigmoid)))


def relay_join(own_part, their_part, is_upper, join_axis):
    lower_first = jnp.concatenate([own_part, their_part], axis=join_axis)
    upper_first = jnp.concatenate([their_part, own_part], axis=join_axis)
    return jnp.where(is_upper, upper_first, lower_first)


def add_round(own_part, their_part):
    return (own_part.astype(F32) + their_part.astype(F32)).astype(BF)


def reorder(rows, key, parts):
    blocks = rows.reshape(parts, rows.shape[0] // parts, rows.shape[1])
    return jnp.concatenate(
        [lax.dynamic_index_in_dim(blocks, key ^ i, 0, keepdims=False) for i in range(parts)], axis=0
    )


def all_to_all(rows, experts):
    moved = lax.all_to_all(
        rows.reshape(experts, rows.shape[0] // experts, rows.shape[1]),
        "expert",
        split_axis=0,
        concat_axis=0,
        tiled=True,
    )
    return moved.reshape(rows.shape)


def pair_core(rows):
    n = rows.shape[0] // 2
    return rows[:n], swap(rows[n:], "expert", 1)


def to_chips(own, other):
    n = own.shape[0] // 4
    blocks = [
        jnp.concatenate([own[m * n:(m + 1) * n], other[m * n:(m + 1) * n]], axis=0) for m in range(4)
    ]
    return jnp.concatenate(
        [blocks[0]] + [swap(blocks[m], "expert", 2 * m) for m in range(1, 4)], axis=0
    )


def from_chips(rows, *earlier):
    n = rows.shape[0] // 8
    blocks = [rows[2 * m * n:2 * (m + 1) * n] for m in range(4)]
    back = after([blocks[0]] + [swap(blocks[m], "expert", 2 * m) for m in range(1, 4)], *earlier)
    other = swap(jnp.concatenate([each[n:] for each in back], axis=0), "expert", 1)
    return jnp.concatenate([each[:n] for each in back] + [other], axis=0)


def scatter_far(first, second):
    n = first.shape[0] // 4
    via_x = swap(first[3 * n:], "dp", 1)
    via_y = swap(second[3 * n:], "dp", 2)
    to_x = jnp.concatenate([first[n:2 * n], add_round(second[n:2 * n], via_y)], axis=1)
    to_y = jnp.concatenate([add_round(first[2 * n:3 * n], via_x), second[2 * n:3 * n]], axis=1)
    return to_x, to_y


def scatter_near(first, second, to_x, to_y):
    n = first.shape[0] // 4
    c = first.shape[1]
    from_x = swap(to_x, "dp", 1)
    from_y = swap(to_y, "dp", 2)
    return tuple(
        own[:n].astype(F32) + x.astype(F32) + y.astype(F32)
        for own, x, y in ((first, from_x[:, :c], from_y[:, :c]), (second, from_x[:, c:], from_y[:, c:]))
    )


def gather_near(first, second):
    own = jnp.concatenate([first, second], axis=1)
    return swap(own, "dp", 1), swap(own, "dp", 2)


def gather_far(first, second, from_x, from_y):
    c = first.shape[1]
    far_first = swap(from_y[:, :c], "dp", 1)
    far_second = swap(from_x[:, c:], "dp", 2)
    return (
        jnp.concatenate([first, from_x[:, :c], from_y[:, :c], far_first], axis=0),
        jnp.concatenate([second, from_x[:, c:], from_y[:, c:], far_second], axis=0),
    )


CONTRACT_FEATS = (((1,), (1,)), ((), ()))
CONTRACT_ROWS = (((0,), (0,)), ((), ()))


def per_device(tokens, expert_ids, route_weights, w_gate, w_up, w_down, out_grad):
    experts = lax.axis_size("expert")
    copies = experts // 8
    levels = copies.bit_length() - 1
    owner_index = lax.axis_index("expert")
    me = lax.axis_index("dp")
    copy_index = owner_index % copies
    tok_rows = tokens.shape[0]
    shard_width = w_gate.shape[0]
    capacity = max(2, 5 * tok_rows // (2 * experts))
    buckets = experts * capacity
    near = experts <= 8
    keys = expert_ids
    if near:
        keys = expert_ids ^ owner_index
        keys = (keys & 1) * 4 + (keys >> 1)

    lanes = jnp.arange(experts, dtype=jnp.int32)[None, :]
    first = keys[:, :1] == lanes
    second = keys[:, 1:] == lanes
    named = (first | second).astype(BF)
    earlier = (
        jnp.arange(tok_rows, dtype=jnp.int32)[None, :] < jnp.arange(tok_rows, dtype=jnp.int32)[:, None]
    ).astype(BF)
    before = jnp.dot(earlier, named, preferred_element_type=F32)
    slots = jnp.arange(buckets, dtype=jnp.int32)[None, :]

    def place(chosen, key):
        rank = jnp.sum(jnp.where(chosen, before, 0.0), axis=1, keepdims=True).astype(jnp.int32)
        return (slots == key * capacity + rank).astype(BF)

    place_0 = place(first, keys[:, :1])
    place_1 = place(second, keys[:, 1:])
    send_rows = lax.dot_general(
        place_0 + place_1, tokens, CONTRACT_ROWS, preferred_element_type=F32
    ).astype(BF)
    grad_f32 = out_grad.astype(F32)
    cot_0 = (route_weights[:, :1] * grad_f32).astype(BF)
    cot_1 = (route_weights[:, 1:] * grad_f32).astype(BF)
    cot_send = (
        lax.dot_general(place_0, cot_0, CONTRACT_ROWS, preferred_element_type=F32)
        + lax.dot_general(place_1, cot_1, CONTRACT_ROWS, preferred_element_type=F32)
    ).astype(BF)
    if near:
        in_rows = reorder(to_chips(*pair_core(send_rows)), me, 4)
        own_cot, other_cot = pair_core(cot_send)
        own_cot, other_cot = after((own_cot, other_cot), in_rows)
        cot_rows = reorder(to_chips(own_cot, other_cot), me, 4)
    else:
        in_rows = reorder(all_to_all(send_rows, experts), me, 4)
        cot_rows = reorder(all_to_all(cot_send, experts), me, 4)

    pieces = (w_gate, w_up, w_down)
    for bit_index in range(levels):
        partner = from_partner(as_sent(pieces), "expert", bit_index)
        is_upper = owner_index // 2**bit_index % 2 == 1
        pieces = tuple(relay_join(own, their, is_upper, 0) for own, their in zip(pieces, partner))
    gate_w, up_w, down_w = pieces

    def partial_product(rows, weights):
        return lax.dot_general(rows, weights, CONTRACT_FEATS, preferred_element_type=F32).astype(BF)

    half = gate_w.shape[0] // 2
    part_gate, part_up = partial_product(in_rows, gate_w), partial_product(in_rows, up_w)
    to_x, to_y = scatter_far(part_gate, part_up)
    gate_sum, up_sum = scatter_near(part_gate, part_up, to_x, to_y)
    cot_rows = after(cot_rows, gate_sum, up_sum)

    active, slope_term = silu_parts(gate_sum)
    own_hidden = (active * up_sum).astype(BF)
    own_hidden = (own_hidden[:, :half], own_hidden[:, half:])
    near_hidden = gather_near(*own_hidden)

    part_hidden = partial_product(cot_rows, down_w)
    part_first, part_second = part_hidden[:, :half], part_hidden[:, half:]
    to_x, to_y = scatter_far(part_first, part_second)
    to_x, to_y = after((to_x, to_y), near_hidden)
    hidden = jnp.concatenate(gather_far(*own_hidden, *near_hidden), axis=1)
    grad_hidden = jnp.concatenate(scatter_near(part_first, part_second, to_x, to_y), axis=1)
    out_rows = jnp.dot(hidden, down_w, preferred_element_type=F32).astype(BF)

    own_grads = ((grad_hidden * up_sum * slope_term).astype(BF), (grad_hidden * active).astype(BF))
    near_grads = gather_near(*own_grads)
    grad_gate_rows, grad_up_rows = gather_far(*own_grads, *near_grads)

    if near:
        returned = from_chips(reorder(out_rows, me, 4), near_grads)
    else:
        returned = all_to_all(reorder(out_rows, me, 4), experts)
    picked_0 = jnp.dot(place_0, returned, preferred_element_type=F32)
    picked_1 = jnp.dot(place_1, returned, preferred_element_type=F32)
    output = (route_weights[:, :1] * picked_0 + route_weights[:, 1:] * picked_1).astype(BF)

    def term(left, right):
        return lax.dot_general(left, right, CONTRACT_ROWS, preferred_element_type=F32).astype(BF)

    grad_terms = (term(grad_gate_rows, in_rows), term(grad_up_rows, in_rows), term(hidden, cot_rows))
    for bit_index in range(levels):
        partner = from_partner(grad_terms, "expert", bit_index)
        grad_terms = tuple(add_round(own, their) for own, their in zip(grad_terms, partner))
    start_row = copy_index * shard_width
    grads = [lax.dynamic_slice_in_dim(each, start_row, shard_width, 0) for each in grad_terms]
    return (output, *grads)


def solution(mesh):
    split = P("expert", "dp")
    pairs = P("expert", None)
    return jax.shard_map(
        per_device,
        mesh=mesh,
        in_specs=(split, pairs, pairs, split, split, split, split),
        out_specs=(split, split, split, split),
        check_vma=False,
    )
```

```python
import jax
import jax.numpy as jnp
from jax import lax
from jax.sharding import PartitionSpec as P

BF = jnp.bfloat16
F32 = jnp.float32


def as_sent(array):

    def short(part):
        return part.astype(BF) if part.dtype == F32 else part

    return jax.tree.map(short, array)


def from_partner(block, axis, bit):
    count = lax.axis_size(axis)
    route = []
    for low in range(count):
        high = low | 1 << bit
        if high != low and high < count:
            route += [(low, high), (high, low)]
    return lax.ppermute(block, axis, route)


def swap(block, axis, mask):
    count = lax.axis_size(axis)
    return lax.ppermute(block, axis, [(i, i ^ mask) for i in range(count)])


def after(values):
    return lax.optimization_barrier(values)


def silu_parts(gate_sum):
    gate_sigmoid = jax.nn.sigmoid(gate_sum)
    return (gate_sum * gate_sigmoid, gate_sigmoid * (1.0 + gate_sum * (1.0 - gate_sigmoid)))


def relay_join(own_part, their_part, is_upper, join_axis):
    lower_first = jnp.concatenate([own_part, their_part], axis=join_axis)
    upper_first = jnp.concatenate([their_part, own_part], axis=join_axis)
    return jnp.where(is_upper, upper_first, lower_first)


def add_round(own_part, their_part):
    return (own_part.astype(F32) + their_part.astype(F32)).astype(BF)


def reorder(rows, key, parts):
    blocks = rows.reshape(parts, rows.shape[0] // parts, rows.shape[1])
    return jnp.concatenate(
        [lax.dynamic_index_in_dim(blocks, key ^ i, 0, keepdims=False) for i in range(parts)], axis=0
    )


def all_to_all(rows, experts):
    moved = lax.all_to_all(
        rows.reshape(experts, rows.shape[0] // experts, rows.shape[1]),
        "expert",
        split_axis=0,
        concat_axis=0,
        tiled=True,
    )
    return moved.reshape(rows.shape)


def pair_core(rows):
    n = rows.shape[0] // 2
    return rows[:n], swap(rows[n:], "expert", 1)


def to_chips(own, other):
    n = own.shape[0] // 4
    blocks = [
        jnp.concatenate([own[m * n:(m + 1) * n], other[m * n:(m + 1) * n]], axis=0) for m in range(4)
    ]
    return jnp.concatenate(
        [blocks[0]] + [swap(blocks[m], "expert", 2 * m) for m in range(1, 4)], axis=0
    )


def swap_places(rows):
    n = rows.shape[0] // 8
    return rows.reshape(2, 4, n, rows.shape[1]).swapaxes(0, 1).reshape(rows.shape)


def swap_back(rows):
    n = rows.shape[0] // 8
    return rows.reshape(4, 2, n, rows.shape[1]).swapaxes(0, 1).reshape(rows.shape)


def scatter_far(part):
    n, c = part.shape[0] // 4, part.shape[1] // 2
    via_x = swap(part[3 * n:, :c], "dp", 1)
    via_y = swap(part[3 * n:, c:], "dp", 2)
    to_x = jnp.concatenate([part[n:2 * n, :c], add_round(part[n:2 * n, c:], via_y)], axis=1)
    to_y = jnp.concatenate([add_round(part[2 * n:3 * n, :c], via_x), part[2 * n:3 * n, c:]], axis=1)
    return to_x, to_y


def scatter_near(part, to_x, to_y):
    n = part.shape[0] // 4
    return part[:n].astype(F32) + swap(to_x, "dp", 1).astype(F32) + swap(to_y, "dp", 2).astype(F32)


def gather_near(own):
    return swap(own, "dp", 1), swap(own, "dp", 2)


def gather_far(own, from_x, from_y):
    c = own.shape[1] // 2
    far_first = swap(from_y[:, :c], "dp", 1)
    far_second = swap(from_x[:, c:], "dp", 2)
    return jnp.concatenate([own, from_x, from_y, jnp.concatenate([far_first, far_second], axis=1)], axis=0)


CONTRACT_FEATS = (((1,), (1,)), ((), ()))
CONTRACT_ROWS = (((0,), (0,)), ((), ()))


def per_device(tokens, expert_ids, route_weights, w_gate, w_up, w_down, out_grad):
    experts = lax.axis_size("expert")
    copies = experts // 8
    levels = copies.bit_length() - 1
    owner_index = lax.axis_index("expert")
    me = lax.axis_index("dp")
    copy_index = owner_index % copies
    tok_rows = tokens.shape[0]
    shard_width = w_gate.shape[0]
    capacity = max(2, 5 * tok_rows // (2 * experts))
    buckets = experts * capacity
    near = experts <= 8
    keys = expert_ids
    if near:
        keys = expert_ids ^ owner_index
        keys = (keys & 1) * 4 + (keys >> 1)

    lanes = jnp.arange(experts, dtype=jnp.int32)[None, :]
    first = keys[:, :1] == lanes
    second = keys[:, 1:] == lanes
    named = (first | second).astype(BF)
    earlier = (
        jnp.arange(tok_rows, dtype=jnp.int32)[None, :] < jnp.arange(tok_rows, dtype=jnp.int32)[:, None]
    ).astype(BF)
    before = jnp.dot(earlier, named, preferred_element_type=F32)
    slots = jnp.arange(buckets, dtype=jnp.int32)[None, :]

    def place(chosen, key):
        rank = jnp.sum(jnp.where(chosen, before, 0.0), axis=1, keepdims=True).astype(jnp.int32)
        return (slots == key * capacity + rank).astype(BF)

    place_0 = place(first, keys[:, :1])
    place_1 = place(second, keys[:, 1:])
    send_rows = lax.dot_general(
        place_0 + place_1, tokens, CONTRACT_ROWS, preferred_element_type=F32
    ).astype(BF)
    grad_f32 = out_grad.astype(F32)
    cot_0 = (route_weights[:, :1] * grad_f32).astype(BF)
    cot_1 = (route_weights[:, 1:] * grad_f32).astype(BF)
    cot_send = (
        lax.dot_general(place_0, cot_0, CONTRACT_ROWS, preferred_element_type=F32)
        + lax.dot_general(place_1, cot_1, CONTRACT_ROWS, preferred_element_type=F32)
    ).astype(BF)
    if near:
        in_rows = reorder(to_chips(*pair_core(send_rows)), me, 4)
        cot_send = reorder(swap_places(cot_send), owner_index, 8)
    else:
        in_rows = reorder(all_to_all(send_rows, experts), me, 4)

    pieces = (w_gate, w_up, w_down)
    for bit_index in range(levels):
        partner = from_partner(as_sent(pieces), "expert", bit_index)
        is_upper = owner_index // 2**bit_index % 2 == 1
        pieces = tuple(relay_join(own, their, is_upper, 0) for own, their in zip(pieces, partner))
    gate_w, up_w, down_w = pieces

    def partial_product(rows, weights):
        return lax.dot_general(rows, weights, CONTRACT_FEATS, preferred_element_type=F32).astype(BF)

    part_gate, part_up = partial_product(in_rows, gate_w), partial_product(in_rows, up_w)
    way_gate, way_up = scatter_far(part_gate), scatter_far(part_up)
    cot_send, way_up = after((cot_send, way_up))
    cot_rows = all_to_all(cot_send, experts)
    gate_sum, up_sum = scatter_near(part_gate, *way_gate), scatter_near(part_up, *way_up)
    active, slope_term = silu_parts(gate_sum)
    own_hidden = (active * up_sum).astype(BF)
    near_hidden = gather_near(own_hidden)

    cot_rows, near_hidden = after((cot_rows, near_hidden))
    if near:
        cot_rows = reorder(cot_rows, owner_index ^ (2 * me), 8)
    else:
        cot_rows = reorder(cot_rows, me, 4)
    part = partial_product(cot_rows, down_w)
    on_way = scatter_far(part)
    hidden = gather_far(own_hidden, *near_hidden)
    out_rows = jnp.dot(hidden, down_w, preferred_element_type=F32).astype(BF)
    grad_hidden = scatter_near(part, *on_way)

    own_gate = (grad_hidden * up_sum * slope_term).astype(BF)
    own_up = (grad_hidden * active).astype(BF)
    near_gate, near_up = gather_near(own_gate), gather_near(own_up)
    if near:
        returned = all_to_all(reorder(out_rows, owner_index ^ (2 * me), 8), experts)
    else:
        returned = all_to_all(reorder(out_rows, me, 4), experts)
    hidden, returned, near_gate = after((hidden, returned, near_gate))
    if near:
        returned = swap_back(reorder(returned, owner_index, 8))
    gate_rows = gather_far(own_gate, *near_gate)
    up_rows = gather_far(own_up, *near_up)
    picked_0 = jnp.dot(place_0, returned, preferred_element_type=F32)
    picked_1 = jnp.dot(place_1, returned, preferred_element_type=F32)
    output = (route_weights[:, :1] * picked_0 + route_weights[:, 1:] * picked_1).astype(BF)

    def term(left, right):
        return lax.dot_general(left, right, CONTRACT_ROWS, preferred_element_type=F32).astype(BF)

    grad_terms = (term(gate_rows, in_rows), term(up_rows, in_rows), term(hidden, cot_rows))
    for bit_index in range(levels):
        partner = from_partner(grad_terms, "expert", bit_index)
        grad_terms = tuple(add_round(own, their) for own, their in zip(grad_terms, partner))
    start_row = copy_index * shard_width
    grads = [lax.dynamic_slice_in_dim(each, start_row, shard_width, 0) for each in grad_terms]
    return (output, *grads)


def solution(mesh):
    split = P("expert", "dp")
    pairs = P("expert", None)
    return jax.shard_map(
        per_device,
        mesh=mesh,
        in_specs=(split, pairs, pairs, split, split, split, split),
        out_specs=(split, split, split, split),
        check_vma=False,
    )
```

```python
import jax
import jax.numpy as jnp
from jax import lax
from jax.sharding import PartitionSpec as P

BF = jnp.bfloat16
F32 = jnp.float32


def as_sent(array):

    def short(part):
        return part.astype(BF) if part.dtype == F32 else part

    return jax.tree.map(short, array)


def from_partner(block, axis, bit):
    count = lax.axis_size(axis)
    route = []
    for low in range(count):
        high = low | 1 << bit
        if high != low and high < count:
            route += [(low, high), (high, low)]
    return lax.ppermute(block, axis, route)


def swap(block, axis, mask):
    count = lax.axis_size(axis)
    return lax.ppermute(block, axis, [(i, i ^ mask) for i in range(count)])


def after(values):
    return lax.optimization_barrier(values)


def after_start(value, earlier):
    value, column = after((value, earlier))
    return value, 0.0 * column.astype(F32)


def silu_parts(gate_sum):
    gate_sigmoid = jax.nn.sigmoid(gate_sum)
    return (gate_sum * gate_sigmoid, gate_sigmoid * (1.0 + gate_sum * (1.0 - gate_sigmoid)))


def relay_join(own_part, their_part, is_upper, join_axis):
    lower_first = jnp.concatenate([own_part, their_part], axis=join_axis)
    upper_first = jnp.concatenate([their_part, own_part], axis=join_axis)
    return jnp.where(is_upper, upper_first, lower_first)


def add_round(own_part, their_part):
    return (own_part.astype(F32) + their_part.astype(F32)).astype(BF)


def reorder(rows, key, parts):
    blocks = rows.reshape(parts, rows.shape[0] // parts, rows.shape[1])
    return jnp.concatenate(
        [lax.dynamic_index_in_dim(blocks, key ^ i, 0, keepdims=False) for i in range(parts)], axis=0
    )


def all_to_all(rows, experts):
    moved = lax.all_to_all(
        rows.reshape(experts, rows.shape[0] // experts, rows.shape[1]),
        "expert",
        split_axis=0,
        concat_axis=0,
        tiled=True,
    )
    return moved.reshape(rows.shape)


def pair_core(rows):
    n = rows.shape[0] // 2
    return rows[:n], swap(rows[n:], "expert", 1)


def to_chips(own, other):
    n = own.shape[0] // 4
    blocks = [
        jnp.concatenate([own[m * n:(m + 1) * n], other[m * n:(m + 1) * n]], axis=0) for m in range(4)
    ]
    return [blocks[0]] + [swap(blocks[m], "expert", 2 * m) for m in range(1, 4)]


def to_chips_first(rows):
    n = rows.shape[0] // 8
    blocks = [
        jnp.concatenate([rows[m * n:(m + 1) * n], rows[(4 + m) * n:(5 + m) * n]], axis=0) for m in range(4)
    ]
    return [blocks[0]] + [swap(blocks[m], "expert", 2 * m) for m in range(1, 4)]


def core_last(got):
    n = got[0].shape[0] // 2
    other = swap(jnp.concatenate([each[n:] for each in got], axis=0), "expert", 1)
    rows = []
    for m, each in enumerate(got):
        rows += [each[:n], other[m * n:(m + 1) * n]]
    return rows


def from_chips(rows):
    n = rows.shape[0] // 4
    return [rows[:n]] + [swap(rows[m * n:(m + 1) * n], "expert", 2 * m) for m in range(1, 4)]


def from_core(back):
    n = back[0].shape[0] // 2
    other = swap(jnp.concatenate([each[n:] for each in back], axis=0), "expert", 1)
    return jnp.concatenate([each[:n] for each in back] + [other], axis=0)


def scatter_far(first, second):
    n = first.shape[0] // 4
    return swap(first[3 * n:], "dp", 1), swap(second[3 * n:], "dp", 2)


def scatter_add(first, second, via_x, via_y):
    n = first.shape[0] // 4
    to_x = jnp.concatenate([first[n:2 * n], add_round(second[n:2 * n], via_y)], axis=1)
    to_y = jnp.concatenate([add_round(first[2 * n:3 * n], via_x), second[2 * n:3 * n]], axis=1)
    return to_x, to_y


def scatter_near(first, second, to_x, to_y):
    n = first.shape[0] // 4
    c = first.shape[1]
    from_x = swap(to_x, "dp", 1)
    from_y = swap(to_y, "dp", 2)
    return tuple(
        own[:n].astype(F32) + x.astype(F32) + y.astype(F32)
        for own, x, y in ((first, from_x[:, :c], from_y[:, :c]), (second, from_x[:, c:], from_y[:, c:]))
    )


def gather_near(first, second):
    own = jnp.concatenate([first, second], axis=1)
    return swap(own, "dp", 1), swap(own, "dp", 2)


def gather_far(first, second, from_x, from_y):
    c = first.shape[1]
    far_first = swap(from_y[:, :c], "dp", 1)
    far_second = swap(from_x[:, c:], "dp", 2)
    return (
        jnp.concatenate([first, from_x[:, :c], from_y[:, :c], far_first], axis=0),
        jnp.concatenate([second, from_x[:, c:], from_y[:, c:], far_second], axis=0),
    )


CONTRACT_FEATS = (((1,), (1,)), ((), ()))
CONTRACT_ROWS = (((0,), (0,)), ((), ()))


def per_device(tokens, expert_ids, route_weights, w_gate, w_up, w_down, out_grad):
    experts = lax.axis_size("expert")
    copies = experts // 8
    levels = copies.bit_length() - 1
    owner_index = lax.axis_index("expert")
    me = lax.axis_index("dp")
    copy_index = owner_index % copies
    tok_rows = tokens.shape[0]
    shard_width = w_gate.shape[0]
    capacity = max(2, 5 * tok_rows // (2 * experts))
    buckets = experts * capacity
    near = experts <= 8
    keys = expert_ids
    if near:
        keys = expert_ids ^ owner_index
        keys = (keys & 1) * 4 + (keys >> 1)

    lanes = jnp.arange(experts, dtype=jnp.int32)[None, :]
    first = keys[:, :1] == lanes
    second = keys[:, 1:] == lanes
    named = (first | second).astype(BF)
    earlier = (
        jnp.arange(tok_rows, dtype=jnp.int32)[None, :] < jnp.arange(tok_rows, dtype=jnp.int32)[:, None]
    ).astype(BF)
    before = jnp.dot(earlier, named, preferred_element_type=F32)
    slots = jnp.arange(buckets, dtype=jnp.int32)[None, :]

    def place(chosen, key):
        rank = jnp.sum(jnp.where(chosen, before, 0.0), axis=1, keepdims=True).astype(jnp.int32)
        return (slots == key * capacity + rank).astype(BF)

    place_0 = place(first, keys[:, :1])
    place_1 = place(second, keys[:, 1:])
    send_rows = lax.dot_general(
        place_0 + place_1, tokens, CONTRACT_ROWS, preferred_element_type=F32
    ).astype(BF)
    grad_f32 = out_grad.astype(F32)
    cot_0 = (route_weights[:, :1] * grad_f32).astype(BF)
    cot_1 = (route_weights[:, 1:] * grad_f32).astype(BF)
    cot_send = (
        lax.dot_general(place_0, cot_0, CONTRACT_ROWS, preferred_element_type=F32)
        + lax.dot_general(place_1, cot_1, CONTRACT_ROWS, preferred_element_type=F32)
    ).astype(BF)
    if near:
        in_rows = to_chips(*pair_core(send_rows))
        cot_send, in_rows = after((cot_send, in_rows))
        cot_rows = to_chips_first(cot_send)
    else:
        in_rows = [all_to_all(send_rows, experts)]
        cot_rows = [all_to_all(cot_send, experts)]
    in_rows = reorder(jnp.concatenate(in_rows, axis=0), me, 4)

    pieces = (w_gate, w_up, w_down)
    for bit_index in range(levels):
        partner = from_partner(as_sent(pieces), "expert", bit_index)
        is_upper = owner_index // 2**bit_index % 2 == 1
        pieces = tuple(relay_join(own, their, is_upper, 0) for own, their in zip(pieces, partner))
    gate_w, up_w, down_w = pieces

    def partial_product(rows, weights):
        return lax.dot_general(rows, weights, CONTRACT_FEATS, preferred_element_type=F32).astype(BF)

    half = gate_w.shape[0] // 2
    part_gate, part_up = partial_product(in_rows, gate_w), partial_product(in_rows, up_w)
    to_x, to_y = scatter_add(part_gate, part_up, *scatter_far(part_gate, part_up))
    gate_sum, up_sum = scatter_near(part_gate, part_up, to_x, to_y)
    cot_rows, zeros = after_start(cot_rows, to_x[:, -1:] + to_y[:, :1])
    if near:
        cot_rows = core_last(cot_rows)
    cot_rows = reorder(jnp.concatenate(cot_rows, axis=0), me, 4)

    active, slope_term = silu_parts(gate_sum)
    own_hidden = (active * up_sum).astype(BF)

    part_hidden = partial_product(cot_rows, down_w)
    part_first, part_second = part_hidden[:, :half], part_hidden[:, half:]
    via, more_zeros = after_start(scatter_far(part_first, part_second), own_hidden[:, :1])
    to_x, to_y = scatter_add(part_first, part_second, *via)
    own_hidden = (own_hidden[:, :half], own_hidden[:, half:])
    near_hidden = gather_near(*own_hidden)
    hidden = jnp.concatenate(gather_far(*own_hidden, *near_hidden), axis=1)
    grad_hidden = jnp.concatenate(scatter_near(part_first, part_second, to_x, to_y), axis=1) + zeros + more_zeros
    out_rows = jnp.dot(hidden, down_w, preferred_element_type=F32).astype(BF)

    own_grads = ((grad_hidden * up_sum * slope_term).astype(BF), (grad_hidden * active).astype(BF))
    hidden, near_grads = after((hidden, gather_near(*own_grads)))
    grad_rows = gather_far(*own_grads, *near_grads)
    back = reorder(out_rows, me, 4)
    if near:
        back, grad_rows = after((from_chips(back), grad_rows))
        returned = from_core(back)
    else:
        returned = all_to_all(back, experts)
    picked_0 = jnp.dot(place_0, returned, preferred_element_type=F32)
    picked_1 = jnp.dot(place_1, returned, preferred_element_type=F32)
    output = (route_weights[:, :1] * picked_0 + route_weights[:, 1:] * picked_1).astype(BF)

    def term(left, right):
        return lax.dot_general(left, right, CONTRACT_ROWS, preferred_element_type=F32).astype(BF)

    grad_terms = (term(grad_rows[0], in_rows), term(grad_rows[1], in_rows), term(hidden, cot_rows))
    for bit_index in range(levels):
        partner = from_partner(grad_terms, "expert", bit_index)
        grad_terms = tuple(add_round(own, their) for own, their in zip(grad_terms, partner))
    start_row = copy_index * shard_width
    grads = [lax.dynamic_slice_in_dim(each, start_row, shard_width, 0) for each in grad_terms]
    return (output, *grads)


def solution(mesh):
    split = P("expert", "dp")
    pairs = P("expert", None)
    return jax.shard_map(
        per_device,
        mesh=mesh,
        in_specs=(split, pairs, pairs, split, split, split, split),
        out_specs=(split, split, split, split),
        check_vma=False,
    )
```

```python
import jax
import jax.numpy as jnp
from jax import lax
from jax.sharding import PartitionSpec as P

BF = jnp.bfloat16
F32 = jnp.float32


def as_sent(array):

    def short(part):
        return part.astype(BF) if part.dtype == F32 else part

    return jax.tree.map(short, array)


def from_partner(block, axis, bit):
    count = lax.axis_size(axis)
    route = []
    for low in range(count):
        high = low | 1 << bit
        if high != low and high < count:
            route += [(low, high), (high, low)]
    return lax.ppermute(block, axis, route)


def swap(block, axis, mask):
    count = lax.axis_size(axis)
    return lax.ppermute(block, axis, [(i, i ^ mask) for i in range(count)])


def after(values):
    return lax.optimization_barrier(values)


def after_start(value, earlier):
    value, column = after((value, earlier))
    return value, 0.0 * column.astype(F32)


def silu_parts(gate_sum):
    gate_sigmoid = jax.nn.sigmoid(gate_sum)
    return (gate_sum * gate_sigmoid, gate_sigmoid * (1.0 + gate_sum * (1.0 - gate_sigmoid)))


def relay_join(own_part, their_part, is_upper, join_axis):
    lower_first = jnp.concatenate([own_part, their_part], axis=join_axis)
    upper_first = jnp.concatenate([their_part, own_part], axis=join_axis)
    return jnp.where(is_upper, upper_first, lower_first)


def add_round(own_part, their_part):
    return (own_part.astype(F32) + their_part.astype(F32)).astype(BF)


def reorder(rows, key, parts):
    blocks = rows.reshape(parts, rows.shape[0] // parts, rows.shape[1])
    return jnp.concatenate(
        [lax.dynamic_index_in_dim(blocks, key ^ i, 0, keepdims=False) for i in range(parts)], axis=0
    )


def all_to_all(rows, experts):
    moved = lax.all_to_all(
        rows.reshape(experts, rows.shape[0] // experts, rows.shape[1]),
        "expert",
        split_axis=0,
        concat_axis=0,
        tiled=True,
    )
    return moved.reshape(rows.shape)


def pair_core(rows):
    n = rows.shape[0] // 2
    return rows[:n], swap(rows[n:], "expert", 1)


def to_chips(own, other):
    n = own.shape[0] // 4
    blocks = [
        jnp.concatenate([own[m * n:(m + 1) * n], other[m * n:(m + 1) * n]], axis=0) for m in range(4)
    ]
    return [blocks[0]] + [swap(blocks[m], "expert", 2 * m) for m in range(1, 4)]


def by_chip(rows):
    n = rows.shape[0] // 8
    blocks = [
        jnp.concatenate([rows[m * n:(m + 1) * n], rows[(4 + m) * n:(5 + m) * n]], axis=0) for m in range(4)
    ]
    return blocks


def core_last(got):
    n = got[0].shape[0] // 2
    other = swap(jnp.concatenate([each[n:] for each in got], axis=0), "expert", 1)
    rows = []
    for m, each in enumerate(got):
        rows += [each[:n], other[m * n:(m + 1) * n]]
    return rows


def from_chips(rows):
    n = rows.shape[0] // 4
    return [rows[:n]] + [swap(rows[m * n:(m + 1) * n], "expert", 2 * m) for m in range(1, 4)]


def from_core(back):
    n = back[0].shape[0] // 2
    other = swap(jnp.concatenate([each[n:] for each in back], axis=0), "expert", 1)
    return jnp.concatenate([each[:n] for each in back] + [other], axis=0)


def scatter_far(first, second):
    n = first.shape[0] // 4
    return swap(first[3 * n:], "dp", 1), swap(second[3 * n:], "dp", 2)


def scatter_add(first, second, via_x, via_y):
    n = first.shape[0] // 4
    to_x = jnp.concatenate([first[n:2 * n], add_round(second[n:2 * n], via_y)], axis=1)
    to_y = jnp.concatenate([add_round(first[2 * n:3 * n], via_x), second[2 * n:3 * n]], axis=1)
    return to_x, to_y


def scatter_near(first, second, to_x, to_y):
    n = first.shape[0] // 4
    c = first.shape[1]
    from_x = swap(to_x, "dp", 1)
    from_y = swap(to_y, "dp", 2)
    return tuple(
        own[:n].astype(F32) + x.astype(F32) + y.astype(F32)
        for own, x, y in ((first, from_x[:, :c], from_y[:, :c]), (second, from_x[:, c:], from_y[:, c:]))
    )


def gather_near(first, second):
    own = jnp.concatenate([first, second], axis=1)
    return swap(own, "dp", 1), swap(own, "dp", 2)


def gather_far(first, second, from_x, from_y):
    c = first.shape[1]
    far_first = swap(from_y[:, :c], "dp", 1)
    far_second = swap(from_x[:, c:], "dp", 2)
    return (
        (jnp.concatenate([first, from_x[:, :c], from_y[:, :c]], axis=0), far_first),
        (jnp.concatenate([second, from_x[:, c:], from_y[:, c:]], axis=0), far_second),
    )


CONTRACT_FEATS = (((1,), (1,)), ((), ()))
CONTRACT_ROWS = (((0,), (0,)), ((), ()))


def row_product(left, right):
    return lax.dot_general(left, right, CONTRACT_ROWS, preferred_element_type=F32)


def per_device(tokens, expert_ids, route_weights, w_gate, w_up, w_down, out_grad):
    experts = lax.axis_size("expert")
    copies = experts // 8
    levels = copies.bit_length() - 1
    owner_index = lax.axis_index("expert")
    me = lax.axis_index("dp")
    copy_index = owner_index % copies
    tok_rows = tokens.shape[0]
    shard_width = w_gate.shape[0]
    capacity = max(2, 5 * tok_rows // (2 * experts))
    buckets = experts * capacity
    near = experts <= 8
    keys = expert_ids
    if near:
        keys = expert_ids ^ owner_index
        keys = (keys & 1) * 4 + (keys >> 1)

    lanes = jnp.arange(experts, dtype=jnp.int32)[None, :]
    first = keys[:, :1] == lanes
    second = keys[:, 1:] == lanes
    named = (first | second).astype(BF)
    earlier = (
        jnp.arange(tok_rows, dtype=jnp.int32)[None, :] < jnp.arange(tok_rows, dtype=jnp.int32)[:, None]
    ).astype(BF)
    before = jnp.dot(earlier, named, preferred_element_type=F32)
    slots = jnp.arange(buckets, dtype=jnp.int32)[None, :]

    def place(chosen, key):
        rank = jnp.sum(jnp.where(chosen, before, 0.0), axis=1, keepdims=True).astype(jnp.int32)
        return (slots == key * capacity + rank).astype(BF)

    place_0 = place(first, keys[:, :1])
    place_1 = place(second, keys[:, 1:])
    send_rows = lax.dot_general(
        place_0 + place_1, tokens, CONTRACT_ROWS, preferred_element_type=F32
    ).astype(BF)
    grad_f32 = out_grad.astype(F32)
    cot_0 = (route_weights[:, :1] * grad_f32).astype(BF)
    cot_1 = (route_weights[:, 1:] * grad_f32).astype(BF)
    cot_send = (
        lax.dot_general(place_0, cot_0, CONTRACT_ROWS, preferred_element_type=F32)
        + lax.dot_general(place_1, cot_1, CONTRACT_ROWS, preferred_element_type=F32)
    ).astype(BF)
    if near:
        in_rows = to_chips(*pair_core(send_rows))
        in_rows[1], first_zeros = after_start(in_rows[1], in_rows[2][:, :1] + in_rows[3][:, :1])
        cot_send, in_rows = after((by_chip(cot_send), in_rows))
        cot_rows = [cot_send[0]] + [swap(cot_send[m], "expert", 2 * m) for m in range(1, 4)]
    else:
        in_rows = [all_to_all(send_rows, experts)]
        cot_rows = [all_to_all(cot_send, experts)]
        first_zeros = 0.0
    in_rows = reorder(jnp.concatenate(in_rows, axis=0), me, 4)

    pieces = (w_gate, w_up, w_down)
    for bit_index in range(levels):
        partner = from_partner(as_sent(pieces), "expert", bit_index)
        is_upper = owner_index // 2**bit_index % 2 == 1
        pieces = tuple(relay_join(own, their, is_upper, 0) for own, their in zip(pieces, partner))
    gate_w, up_w, down_w = pieces

    def partial_product(rows, weights):
        return lax.dot_general(rows, weights, CONTRACT_FEATS, preferred_element_type=F32).astype(BF)

    half = gate_w.shape[0] // 2
    part_gate, part_up = partial_product(in_rows, gate_w), partial_product(in_rows, up_w)
    to_x, to_y = scatter_add(part_gate, part_up, *scatter_far(part_gate, part_up))
    gate_sum, up_sum = scatter_near(part_gate, part_up, to_x, to_y)
    cot_rows, zeros = after_start(cot_rows, to_x[:, -1:] + to_y[:, :1])
    if near:
        cot_rows = core_last(cot_rows)
    cot_rows = reorder(jnp.concatenate(cot_rows, axis=0), me, 4)

    active, slope_term = silu_parts(gate_sum)
    own_hidden = (active * up_sum).astype(BF)

    part_hidden = partial_product(cot_rows, down_w)
    part_first, part_second = part_hidden[:, :half], part_hidden[:, half:]
    via, more_zeros = after_start(scatter_far(part_first, part_second), own_hidden[:, :1])
    to_x, to_y = scatter_add(part_first, part_second, *via)
    own_hidden = (own_hidden[:, :half], own_hidden[:, half:])
    near_hidden = gather_near(*own_hidden)
    hidden = jnp.concatenate(
        [jnp.concatenate(each, axis=0) for each in gather_far(*own_hidden, *near_hidden)], axis=1
    )
    grad_hidden = jnp.concatenate(scatter_near(part_first, part_second, to_x, to_y), axis=1) + first_zeros + zeros + more_zeros
    out_rows = jnp.dot(hidden, down_w, preferred_element_type=F32).astype(BF)

    own_grads = ((grad_hidden * up_sum * slope_term).astype(BF), (grad_hidden * active).astype(BF))
    down_term, near_grads = after((row_product(hidden, cot_rows).astype(BF), gather_near(*own_grads)))
    grad_rows = gather_far(*own_grads, *near_grads)
    ready = 3 * (in_rows.shape[0] // 4)
    near_terms = [row_product(near_rows, in_rows[:ready]) for near_rows, _ in grad_rows]
    near_terms, far_rows = after((near_terms, [far_rows for _, far_rows in grad_rows]))
    back = reorder(out_rows, me, 4)
    if near:
        back, far_rows = after((from_chips(back), far_rows))
        returned = from_core(back)
    else:
        returned = all_to_all(back, experts)
    picked_0 = jnp.dot(place_0, returned, preferred_element_type=F32)
    picked_1 = jnp.dot(place_1, returned, preferred_element_type=F32)
    output = (route_weights[:, :1] * picked_0 + route_weights[:, 1:] * picked_1).astype(BF)

    grad_terms = [near + row_product(far_rows, in_rows[ready:]) for near, far_rows in zip(near_terms, far_rows)]
    grad_terms = tuple(each.astype(BF) for each in (*grad_terms, down_term))
    for bit_index in range(levels):
        partner = from_partner(grad_terms, "expert", bit_index)
        grad_terms = tuple(add_round(own, their) for own, their in zip(grad_terms, partner))
    start_row = copy_index * shard_width
    grads = [lax.dynamic_slice_in_dim(each, start_row, shard_width, 0) for each in grad_terms]
    return (output, *grads)


def solution(mesh):
    split = P("expert", "dp")
    pairs = P("expert", None)
    return jax.shard_map(
        per_device,
        mesh=mesh,
        in_specs=(split, pairs, pairs, split, split, split, split),
        out_specs=(split, split, split, split),
        check_vma=False,
    )
```

```python
import jax
import jax.numpy as jnp
from jax import lax
from jax.sharding import PartitionSpec as P

BF = jnp.bfloat16
F32 = jnp.float32


def as_sent(array):

    def short(part):
        return part.astype(BF) if part.dtype == F32 else part

    return jax.tree.map(short, array)


def from_partner(block, axis, bit):
    count = lax.axis_size(axis)
    route = []
    for low in range(count):
        high = low | 1 << bit
        if high != low and high < count:
            route += [(low, high), (high, low)]
    return lax.ppermute(block, axis, route)


def swap(block, axis, mask):
    count = lax.axis_size(axis)
    return lax.ppermute(block, axis, [(i, i ^ mask) for i in range(count)])


def after(values):
    return lax.optimization_barrier(values)


def after_start(value, earlier):
    value, column = after((value, earlier))
    return value, 0.0 * column.astype(F32)


def silu_parts(gate_sum):
    gate_sigmoid = jax.nn.sigmoid(gate_sum)
    return (gate_sum * gate_sigmoid, gate_sigmoid * (1.0 + gate_sum * (1.0 - gate_sigmoid)))


def relay_join(own_part, their_part, is_upper, join_axis):
    lower_first = jnp.concatenate([own_part, their_part], axis=join_axis)
    upper_first = jnp.concatenate([their_part, own_part], axis=join_axis)
    return jnp.where(is_upper, upper_first, lower_first)


def add_round(own_part, their_part):
    return (own_part.astype(F32) + their_part.astype(F32)).astype(BF)


def reorder(rows, key, parts):
    blocks = rows.reshape(parts, rows.shape[0] // parts, rows.shape[1])
    return jnp.concatenate(
        [lax.dynamic_index_in_dim(blocks, key ^ i, 0, keepdims=False) for i in range(parts)], axis=0
    )


def all_to_all(rows, experts):
    moved = lax.all_to_all(
        rows.reshape(experts, rows.shape[0] // experts, rows.shape[1]),
        "expert",
        split_axis=0,
        concat_axis=0,
        tiled=True,
    )
    return moved.reshape(rows.shape)


def pair_core(rows):
    n = rows.shape[0] // 2
    return rows[:n], swap(rows[n:], "expert", 1)


def to_chips(own, other):
    n = own.shape[0] // 4
    blocks = [
        jnp.concatenate([own[m * n:(m + 1) * n], other[m * n:(m + 1) * n]], axis=0) for m in range(4)
    ]
    return [blocks[0]] + [swap(blocks[m], "expert", 2 * m) for m in range(1, 4)]


def by_chip(rows):
    n = rows.shape[0] // 8
    blocks = [
        jnp.concatenate([rows[m * n:(m + 1) * n], rows[(4 + m) * n:(5 + m) * n]], axis=0) for m in range(4)
    ]
    return blocks


def core_last(got):
    n = got[0].shape[0] // 2
    other = swap(jnp.concatenate([each[n:] for each in got], axis=0), "expert", 1)
    rows = []
    for m, each in enumerate(got):
        rows += [each[:n], other[m * n:(m + 1) * n]]
    return rows


def from_chips(rows):
    n = rows.shape[0] // 4
    return [rows[:n]] + [swap(rows[m * n:(m + 1) * n], "expert", 2 * m) for m in range(1, 4)]


def from_core(back):
    n = back[0].shape[0] // 2
    other = swap(jnp.concatenate([each[n:] for each in back], axis=0), "expert", 1)
    return jnp.concatenate([each[:n] for each in back] + [other], axis=0)


def scatter_far(first, second):
    n = first.shape[0] // 4
    return swap(first[3 * n:], "dp", 1), swap(second[3 * n:], "dp", 2)


def scatter_add(first, second, via_x, via_y):
    n = first.shape[0] // 4
    to_x = jnp.concatenate([first[n:2 * n], add_round(second[n:2 * n], via_y)], axis=1)
    to_y = jnp.concatenate([add_round(first[2 * n:3 * n], via_x), second[2 * n:3 * n]], axis=1)
    return to_x, to_y


def scatter_near(first, second, to_x, to_y):
    n = first.shape[0] // 4
    c = first.shape[1]
    from_x = swap(to_x, "dp", 1)
    from_y = swap(to_y, "dp", 2)
    return tuple(
        own[:n].astype(F32) + x.astype(F32) + y.astype(F32)
        for own, x, y in ((first, from_x[:, :c], from_y[:, :c]), (second, from_x[:, c:], from_y[:, c:]))
    )


def gather_near(first, second):
    own = jnp.concatenate([first, second], axis=1)
    return swap(own, "dp", 1), swap(own, "dp", 2)


def gather_far(first, second, from_x, from_y):
    c = first.shape[1]
    far_first = swap(from_y[:, :c], "dp", 1)
    far_second = swap(from_x[:, c:], "dp", 2)
    return (
        jnp.concatenate([first, from_x[:, :c], from_y[:, :c], far_first], axis=0),
        jnp.concatenate([second, from_x[:, c:], from_y[:, c:], far_second], axis=0),
    )


CONTRACT_FEATS = (((1,), (1,)), ((), ()))
CONTRACT_ROWS = (((0,), (0,)), ((), ()))


def per_device(tokens, expert_ids, route_weights, w_gate, w_up, w_down, out_grad):
    experts = lax.axis_size("expert")
    copies = experts // 8
    levels = copies.bit_length() - 1
    owner_index = lax.axis_index("expert")
    me = lax.axis_index("dp")
    copy_index = owner_index % copies
    tok_rows = tokens.shape[0]
    shard_width = w_gate.shape[0]
    capacity = max(2, 5 * tok_rows // (2 * experts))
    buckets = experts * capacity
    near = experts <= 8
    keys = expert_ids
    if near:
        keys = expert_ids ^ owner_index
        keys = (keys & 1) * 4 + (keys >> 1)

    lanes = jnp.arange(experts, dtype=jnp.int32)[None, :]
    first = keys[:, :1] == lanes
    second = keys[:, 1:] == lanes
    named = (first | second).astype(BF)
    earlier = (
        jnp.arange(tok_rows, dtype=jnp.int32)[None, :] < jnp.arange(tok_rows, dtype=jnp.int32)[:, None]
    ).astype(BF)
    before = jnp.dot(earlier, named, preferred_element_type=F32)
    slots = jnp.arange(buckets, dtype=jnp.int32)[None, :]

    def place(chosen, key):
        rank = jnp.sum(jnp.where(chosen, before, 0.0), axis=1, keepdims=True).astype(jnp.int32)
        return (slots == key * capacity + rank).astype(BF)

    place_0 = place(first, keys[:, :1])
    place_1 = place(second, keys[:, 1:])
    send_rows = lax.dot_general(
        place_0 + place_1, tokens, CONTRACT_ROWS, preferred_element_type=F32
    ).astype(BF)
    grad_f32 = out_grad.astype(F32)
    cot_0 = (route_weights[:, :1] * grad_f32).astype(BF)
    cot_1 = (route_weights[:, 1:] * grad_f32).astype(BF)
    cot_send = (
        lax.dot_general(place_0, cot_0, CONTRACT_ROWS, preferred_element_type=F32)
        + lax.dot_general(place_1, cot_1, CONTRACT_ROWS, preferred_element_type=F32)
    ).astype(BF)
    if near:
        in_rows = to_chips(*pair_core(send_rows))
        cot_send, in_rows[1] = after((by_chip(cot_send), in_rows[1]))
        cot_next = swap(cot_send[1], "expert", 2)
        cot_send, in_rows = after((cot_send, in_rows))
        cot_rows = [cot_send[0], cot_next, swap(cot_send[2], "expert", 4), swap(cot_send[3], "expert", 6)]
    else:
        in_rows = [all_to_all(send_rows, experts)]
        cot_rows = [all_to_all(cot_send, experts)]
    in_rows = reorder(jnp.concatenate(in_rows, axis=0), me, 4)

    pieces = (w_gate, w_up, w_down)
    for bit_index in range(levels):
        partner = from_partner(as_sent(pieces), "expert", bit_index)
        is_upper = owner_index // 2**bit_index % 2 == 1
        pieces = tuple(relay_join(own, their, is_upper, 0) for own, their in zip(pieces, partner))
    gate_w, up_w, down_w = pieces

    def partial_product(rows, weights):
        return lax.dot_general(rows, weights, CONTRACT_FEATS, preferred_element_type=F32).astype(BF)

    half = gate_w.shape[0] // 2
    part_gate, part_up = partial_product(in_rows, gate_w), partial_product(in_rows, up_w)
    to_x, to_y = scatter_add(part_gate, part_up, *scatter_far(part_gate, part_up))
    gate_sum, up_sum = scatter_near(part_gate, part_up, to_x, to_y)
    cot_rows, zeros = after_start(cot_rows, to_x[:, -1:] + to_y[:, :1])
    if near:
        cot_rows = core_last(cot_rows)
    cot_rows = reorder(jnp.concatenate(cot_rows, axis=0), me, 4)

    active, slope_term = silu_parts(gate_sum)
    own_hidden = (active * up_sum).astype(BF)

    part_hidden = partial_product(cot_rows, down_w)
    part_first, part_second = part_hidden[:, :half], part_hidden[:, half:]
    via, more_zeros = after_start(scatter_far(part_first, part_second), own_hidden[:, :1])
    to_x, to_y = scatter_add(part_first, part_second, *via)
    own_hidden = (own_hidden[:, :half], own_hidden[:, half:])
    near_hidden = gather_near(*own_hidden)
    hidden = jnp.concatenate(gather_far(*own_hidden, *near_hidden), axis=1)
    grad_hidden = jnp.concatenate(scatter_near(part_first, part_second, to_x, to_y), axis=1) + zeros + more_zeros
    out_rows = jnp.dot(hidden, down_w, preferred_element_type=F32).astype(BF)

    own_grads = ((grad_hidden * up_sum * slope_term).astype(BF), (grad_hidden * active).astype(BF))
    hidden, near_grads = after((hidden, gather_near(*own_grads)))
    grad_rows = gather_far(*own_grads, *near_grads)
    back = reorder(out_rows, me, 4)
    if near:
        back, grad_rows = after((from_chips(back), grad_rows))
        returned = from_core(back)
    else:
        returned = all_to_all(back, experts)
    weighted = (route_weights[:, :1] * place_0 + route_weights[:, 1:] * place_1).astype(BF)
    output = jnp.dot(weighted, returned, preferred_element_type=F32).astype(BF)

    def term(left, right):
        return lax.dot_general(left, right, CONTRACT_ROWS, preferred_element_type=F32).astype(BF)

    grad_terms = (term(grad_rows[0], in_rows), term(grad_rows[1], in_rows), term(hidden, cot_rows))
    for bit_index in range(levels):
        partner = from_partner(grad_terms, "expert", bit_index)
        grad_terms = tuple(add_round(own, their) for own, their in zip(grad_terms, partner))
    start_row = copy_index * shard_width
    grads = [lax.dynamic_slice_in_dim(each, start_row, shard_width, 0) for each in grad_terms]
    return (output, *grads)


def solution(mesh):
    split = P("expert", "dp")
    pairs = P("expert", None)
    return jax.shard_map(
        per_device,
        mesh=mesh,
        in_specs=(split, pairs, pairs, split, split, split, split),
        out_specs=(split, split, split, split),
        check_vma=False,
    )
```

```python
import jax
import jax.numpy as jnp
from jax import lax
from jax.sharding import PartitionSpec as P

BF = jnp.bfloat16
F32 = jnp.float32


def as_sent(array):

    def short(part):
        return part.astype(BF) if part.dtype == F32 else part

    return jax.tree.map(short, array)


def from_partner(block, axis, bit):
    count = lax.axis_size(axis)
    route = []
    for low in range(count):
        high = low | 1 << bit
        if high != low and high < count:
            route += [(low, high), (high, low)]
    return lax.ppermute(block, axis, route)


def swap(block, axis, mask):
    count = lax.axis_size(axis)
    return lax.ppermute(block, axis, [(i, i ^ mask) for i in range(count)])


def after(values):
    return lax.optimization_barrier(values)


def after_start(value, earlier):
    value, column = after((value, earlier))
    return value, 0.0 * column.astype(F32)


def silu_parts(gate_sum):
    gate_sigmoid = jax.nn.sigmoid(gate_sum)
    return (gate_sum * gate_sigmoid, gate_sigmoid * (1.0 + gate_sum * (1.0 - gate_sigmoid)))


def relay_join(own_part, their_part, is_upper, join_axis):
    lower_first = jnp.concatenate([own_part, their_part], axis=join_axis)
    upper_first = jnp.concatenate([their_part, own_part], axis=join_axis)
    return jnp.where(is_upper, upper_first, lower_first)


def add_round(own_part, their_part):
    return (own_part.astype(F32) + their_part.astype(F32)).astype(BF)


def reorder(rows, key, parts):
    blocks = rows.reshape(parts, rows.shape[0] // parts, rows.shape[1])
    return jnp.concatenate(
        [lax.dynamic_index_in_dim(blocks, key ^ i, 0, keepdims=False) for i in range(parts)], axis=0
    )


def all_to_all(rows, experts):
    moved = lax.all_to_all(
        rows.reshape(experts, rows.shape[0] // experts, rows.shape[1]),
        "expert",
        split_axis=0,
        concat_axis=0,
        tiled=True,
    )
    return moved.reshape(rows.shape)


def pair_core(rows):
    n = rows.shape[0] // 2
    return rows[:n], swap(rows[n:], "expert", 1)


def to_chips(own, other):
    n = own.shape[0] // 4
    blocks = [
        jnp.concatenate([own[m * n:(m + 1) * n], other[m * n:(m + 1) * n]], axis=0) for m in range(4)
    ]
    return [blocks[0]] + [swap(blocks[m], "expert", 2 * m) for m in range(1, 4)]


def by_chip(rows):
    n = rows.shape[0] // 8
    blocks = [
        jnp.concatenate([rows[m * n:(m + 1) * n], rows[(4 + m) * n:(5 + m) * n]], axis=0) for m in range(4)
    ]
    return blocks


def core_last(got):
    n = got[0].shape[0] // 2
    other = swap(jnp.concatenate([each[n:] for each in got], axis=0), "expert", 1)
    rows = []
    for m, each in enumerate(got):
        rows += [each[:n], other[m * n:(m + 1) * n]]
    return rows


def from_chips(rows):
    n = rows.shape[0] // 4
    return [rows[:n]] + [swap(rows[m * n:(m + 1) * n], "expert", 2 * m) for m in range(1, 4)]


def from_core(back):
    n = back[0].shape[0] // 2
    other = swap(jnp.concatenate([each[n:] for each in back], axis=0), "expert", 1)
    return jnp.concatenate([each[:n] for each in back] + [other], axis=0)


def join_halves(near_rows, far_rows):
    cols = near_rows.shape[1]
    both = jnp.concatenate([near_rows.reshape(4, -1, cols), far_rows.reshape(4, -1, cols)], axis=1)
    return both.reshape(-1, cols)


def split_halves(rows):
    cols = rows.shape[1]
    near_rows, far_rows = jnp.split(rows.reshape(4, -1, cols), 2, axis=1)
    return near_rows.reshape(-1, cols), far_rows.reshape(-1, cols)


def scatter_half(first, second):
    n = first.shape[0] // 4
    from_x = swap(jnp.concatenate([first[n:2 * n], first[3 * n:]], axis=0), "dp", 1)
    from_y = swap(second[2 * n:], "dp", 2)
    return from_x, from_y


def scatter_quarter(first, second, from_x, from_y, together):
    n = first.shape[0] // 4
    to_x, to_y = add_round(second[n:2 * n], from_y[n:]), add_round(first[2 * n:3 * n], from_x[n:])
    if together:
        to_x, to_y = after((to_x, to_y))
    last_x, last_y = swap(to_x, "dp", 1), swap(to_y, "dp", 2)
    if together:
        last_x, last_y = after((last_x, last_y))
    return tuple(
        own[:n].astype(F32) + one[:n].astype(F32) + other.astype(F32)
        for own, one, other in ((first, from_x, last_y), (second, from_y, last_x))
    )


def gather_near(first, second):
    own = jnp.concatenate([first, second], axis=1)
    return swap(own, "dp", 1), swap(own, "dp", 2)


def gather_far(first, second, from_x, from_y):
    c = first.shape[1]
    far_first = swap(from_y[:, :c], "dp", 1)
    far_second = swap(from_x[:, c:], "dp", 2)
    return (
        jnp.concatenate([first, from_x[:, :c], from_y[:, :c], far_first], axis=0),
        jnp.concatenate([second, from_x[:, c:], from_y[:, c:], far_second], axis=0),
    )


CONTRACT_FEATS = (((1,), (1,)), ((), ()))
CONTRACT_ROWS = (((0,), (0,)), ((), ()))


def per_device(tokens, expert_ids, route_weights, w_gate, w_up, w_down, out_grad):
    experts = lax.axis_size("expert")
    copies = experts // 8
    levels = copies.bit_length() - 1
    owner_index = lax.axis_index("expert")
    me = lax.axis_index("dp")
    copy_index = owner_index % copies
    tok_rows = tokens.shape[0]
    shard_width = w_gate.shape[0]
    capacity = max(2, 5 * tok_rows // (2 * experts))
    buckets = experts * capacity
    near = experts <= 8
    keys = expert_ids
    if near:
        keys = expert_ids ^ owner_index
        keys = (keys & 1) * 4 + (keys >> 1)

    lanes = jnp.arange(experts, dtype=jnp.int32)[None, :]
    first = keys[:, :1] == lanes
    second = keys[:, 1:] == lanes
    named = (first | second).astype(BF)
    earlier = (
        jnp.arange(tok_rows, dtype=jnp.int32)[None, :] < jnp.arange(tok_rows, dtype=jnp.int32)[:, None]
    ).astype(BF)
    before = jnp.dot(earlier, named, preferred_element_type=F32)
    slots = jnp.arange(buckets, dtype=jnp.int32)[None, :]

    def place(chosen, key):
        rank = jnp.sum(jnp.where(chosen, before, 0.0), axis=1, keepdims=True).astype(jnp.int32)
        return (slots == key * capacity + rank).astype(BF)

    place_0 = place(first, keys[:, :1])
    place_1 = place(second, keys[:, 1:])
    send_rows = lax.dot_general(
        place_0 + place_1, tokens, CONTRACT_ROWS, preferred_element_type=F32
    ).astype(BF)
    grad_f32 = out_grad.astype(F32)
    cot_0 = (route_weights[:, :1] * grad_f32).astype(BF)
    cot_1 = (route_weights[:, 1:] * grad_f32).astype(BF)
    cot_send = (
        lax.dot_general(place_0, cot_0, CONTRACT_ROWS, preferred_element_type=F32)
        + lax.dot_general(place_1, cot_1, CONTRACT_ROWS, preferred_element_type=F32)
    ).astype(BF)
    if near:
        in_rows = to_chips(*pair_core(send_rows))
        cot_send, in_rows[1] = after((by_chip(cot_send), in_rows[1]))
        cot_next = swap(cot_send[1], "expert", 2)
    else:
        in_rows = jnp.split(all_to_all(send_rows, experts), 2, axis=0)
        cot_rows = [all_to_all(cot_send, experts)]
    pieces = (w_gate, w_up, w_down)
    for bit_index in range(levels):
        partner = from_partner(as_sent(pieces), "expert", bit_index)
        is_upper = owner_index // 2**bit_index % 2 == 1
        pieces = tuple(relay_join(own, their, is_upper, 0) for own, their in zip(pieces, partner))
    gate_w, up_w, down_w = pieces

    def partial_product(rows, weights):
        return lax.dot_general(rows, weights, CONTRACT_FEATS, preferred_element_type=F32).astype(BF)

    half = gate_w.shape[0] // 2
    n = buckets // 4
    middle = len(in_rows) // 2
    near_rows = reorder(jnp.concatenate(in_rows[:middle], axis=0), me, 4)
    near_parts = partial_product(near_rows, gate_w), partial_product(near_rows, up_w)
    near_parts, far_rows = after((near_parts, in_rows[middle:]))
    if near:
        cot_send, far_rows = after((cot_send, far_rows))
        cot_rows = [cot_send[0], cot_next, swap(cot_send[2], "expert", 4), swap(cot_send[3], "expert", 6)]
    far_rows = reorder(jnp.concatenate(far_rows, axis=0), me, 4)
    in_rows = join_halves(near_rows, far_rows)
    part_gate = join_halves(near_parts[0], partial_product(far_rows, gate_w))
    part_up = join_halves(near_parts[1], partial_product(far_rows, up_w))
    halves = scatter_half(part_gate, part_up)
    gate_sum, up_sum = scatter_quarter(part_gate, part_up, *halves, False)
    cot_rows, zeros = after_start(cot_rows, halves[0][:n, :1] + halves[1][:n, :1])
    if near:
        cot_rows = core_last(cot_rows)
    cot_halves = jnp.split(jnp.concatenate(cot_rows, axis=0), 2, axis=0)
    cot_rows = join_halves(*(reorder(rows, me, 4) for rows in cot_halves))

    active, slope_term = silu_parts(gate_sum)
    own_hidden = (active * up_sum).astype(BF)

    part_hidden = partial_product(cot_rows, down_w)
    part_first, part_second = part_hidden[:, :half], part_hidden[:, half:]
    halves, more_zeros = after_start(scatter_half(part_first, part_second), own_hidden[:, :1])
    own_hidden = (own_hidden[:, :half], own_hidden[:, half:])
    near_hidden = gather_near(*own_hidden)
    hidden = jnp.concatenate(gather_far(*own_hidden, *near_hidden), axis=1)
    grad_hidden = jnp.concatenate(scatter_quarter(part_first, part_second, *halves, True), axis=1) + zeros + more_zeros
    out_rows = jnp.dot(hidden, down_w, preferred_element_type=F32).astype(BF)

    own_grads = ((grad_hidden * up_sum * slope_term).astype(BF), (grad_hidden * active).astype(BF))
    hidden, near_grads = after((hidden, gather_near(*own_grads)))
    grad_rows = gather_far(*own_grads, *near_grads)
    back = jnp.concatenate([reorder(rows, me, 4) for rows in split_halves(out_rows)], axis=0)
    if near:
        back, grad_rows = after((from_chips(back), grad_rows))
        returned = from_core(back)
    else:
        returned = all_to_all(back, experts)
    weighted = (route_weights[:, :1] * place_0 + route_weights[:, 1:] * place_1).astype(BF)
    output = jnp.dot(weighted, returned, preferred_element_type=F32).astype(BF)

    def term(left, right):
        return lax.dot_general(left, right, CONTRACT_ROWS, preferred_element_type=F32).astype(BF)

    grad_terms = (term(grad_rows[0], in_rows), term(grad_rows[1], in_rows), term(hidden, cot_rows))
    for bit_index in range(levels):
        partner = from_partner(grad_terms, "expert", bit_index)
        grad_terms = tuple(add_round(own, their) for own, their in zip(grad_terms, partner))
    start_row = copy_index * shard_width
    grads = [lax.dynamic_slice_in_dim(each, start_row, shard_width, 0) for each in grad_terms]
    return (output, *grads)


def solution(mesh):
    split = P("expert", "dp")
    pairs = P("expert", None)
    return jax.shard_map(
        per_device,
        mesh=mesh,
        in_specs=(split, pairs, pairs, split, split, split, split),
        out_specs=(split, split, split, split),
        check_vma=False,
    )
```

```python
import jax
import jax.numpy as jnp
from jax import lax
from jax.sharding import PartitionSpec as P

BF = jnp.bfloat16
F32 = jnp.float32


def as_sent(array):

    def short(part):
        return part.astype(BF) if part.dtype == F32 else part

    return jax.tree.map(short, array)


def from_partner(block, axis, bit):
    count = lax.axis_size(axis)
    route = []
    for low in range(count):
        high = low | 1 << bit
        if high != low and high < count:
            route += [(low, high), (high, low)]
    return lax.ppermute(block, axis, route)


def swap(block, axis, mask):
    count = lax.axis_size(axis)
    return lax.ppermute(block, axis, [(i, i ^ mask) for i in range(count)])


def after(values):
    return lax.optimization_barrier(values)


def after_start(value, earlier):
    value, column = after((value, earlier))
    return value, 0.0 * column.astype(F32)


def silu_parts(gate_sum):
    gate_sigmoid = jax.nn.sigmoid(gate_sum)
    return (gate_sum * gate_sigmoid, gate_sigmoid * (1.0 + gate_sum * (1.0 - gate_sigmoid)))


def relay_join(own_part, their_part, is_upper, join_axis):
    lower_first = jnp.concatenate([own_part, their_part], axis=join_axis)
    upper_first = jnp.concatenate([their_part, own_part], axis=join_axis)
    return jnp.where(is_upper, upper_first, lower_first)


def add_round(own_part, their_part):
    return (own_part.astype(F32) + their_part.astype(F32)).astype(BF)


def reorder(rows, key, parts):
    blocks = rows.reshape(parts, rows.shape[0] // parts, rows.shape[1])
    return jnp.concatenate(
        [lax.dynamic_index_in_dim(blocks, key ^ i, 0, keepdims=False) for i in range(parts)], axis=0
    )


def all_to_all(rows, experts):
    moved = lax.all_to_all(
        rows.reshape(experts, rows.shape[0] // experts, rows.shape[1]),
        "expert",
        split_axis=0,
        concat_axis=0,
        tiled=True,
    )
    return moved.reshape(rows.shape)


def pair_core(rows):
    n = rows.shape[0] // 2
    return rows[:n], swap(rows[n:], "expert", 1)


def to_chips(own, other):
    n = own.shape[0] // 4
    blocks = [
        jnp.concatenate([own[m * n:(m + 1) * n], other[m * n:(m + 1) * n]], axis=0) for m in range(4)
    ]
    return [blocks[0]] + [swap(blocks[m], "expert", 2 * m) for m in range(1, 4)]


def by_chip(rows):
    n = rows.shape[0] // 8
    blocks = [
        jnp.concatenate([rows[m * n:(m + 1) * n], rows[(4 + m) * n:(5 + m) * n]], axis=0) for m in range(4)
    ]
    return blocks


def core_last(got):
    n = got[0].shape[0] // 2
    other = swap(jnp.concatenate([each[n:] for each in got], axis=0), "expert", 1)
    rows = []
    for m, each in enumerate(got):
        rows += [each[:n], other[m * n:(m + 1) * n]]
    return rows


def from_chips(rows):
    n = rows.shape[0] // 4
    return [rows[:n]] + [swap(rows[m * n:(m + 1) * n], "expert", 2 * m) for m in range(1, 4)]


def from_core(back):
    n = back[0].shape[0] // 2
    other = swap(jnp.concatenate([each[n:] for each in back], axis=0), "expert", 1)
    return jnp.concatenate([each[:n] for each in back] + [other], axis=0)


def join_halves(near_rows, far_rows):
    cols = near_rows.shape[1]
    both = jnp.concatenate([near_rows.reshape(4, -1, cols), far_rows.reshape(4, -1, cols)], axis=1)
    return both.reshape(-1, cols)


def split_halves(rows):
    cols = rows.shape[1]
    near_rows, far_rows = jnp.split(rows.reshape(4, -1, cols), 2, axis=1)
    return near_rows.reshape(-1, cols), far_rows.reshape(-1, cols)


def scatter_far(first, second):
    n = first.shape[0] // 4
    return swap(first[3 * n:], "dp", 1), swap(second[3 * n:], "dp", 2)


def scatter_add(first, second, via_x, via_y):
    n = first.shape[0] // 4
    to_x = jnp.concatenate([first[n:2 * n], add_round(second[n:2 * n], via_y)], axis=1)
    to_y = jnp.concatenate([add_round(first[2 * n:3 * n], via_x), second[2 * n:3 * n]], axis=1)
    return to_x, to_y


def scatter_near(first, second, to_x, to_y):
    n = first.shape[0] // 4
    c = first.shape[1]
    from_x = swap(to_x, "dp", 1)
    from_y = swap(to_y, "dp", 2)
    return tuple(
        own[:n].astype(F32) + x.astype(F32) + y.astype(F32)
        for own, x, y in ((first, from_x[:, :c], from_y[:, :c]), (second, from_x[:, c:], from_y[:, c:]))
    )


def scatter_half(first, second):
    n = first.shape[0] // 4
    from_x = swap(jnp.concatenate([first[n:2 * n], first[3 * n:]], axis=0), "dp", 1)
    from_y = swap(second[2 * n:], "dp", 2)
    return from_x, from_y


def scatter_quarter(first, second, from_x, from_y):
    n = first.shape[0] // 4
    last_x = swap(add_round(second[n:2 * n], from_y[n:]), "dp", 1)
    last_y = swap(add_round(first[2 * n:3 * n], from_x[n:]), "dp", 2)
    return last_x, last_y


def sum_quarter(own, one, other):
    n = other.shape[0]
    return own[:n].astype(F32) + one[:n].astype(F32) + other.astype(F32)


def gather_near(first, second):
    own = jnp.concatenate([first, second], axis=1)
    return swap(own, "dp", 1), swap(own, "dp", 2)


def gather_far(first, second, from_x, from_y):
    c = first.shape[1]
    far_first = swap(from_y[:, :c], "dp", 1)
    far_second = swap(from_x[:, c:], "dp", 2)
    return (
        jnp.concatenate([first, from_x[:, :c], from_y[:, :c], far_first], axis=0),
        jnp.concatenate([second, from_x[:, c:], from_y[:, c:], far_second], axis=0),
    )


CONTRACT_FEATS = (((1,), (1,)), ((), ()))
CONTRACT_ROWS = (((0,), (0,)), ((), ()))


def per_device(tokens, expert_ids, route_weights, w_gate, w_up, w_down, out_grad):
    experts = lax.axis_size("expert")
    copies = experts // 8
    levels = copies.bit_length() - 1
    owner_index = lax.axis_index("expert")
    me = lax.axis_index("dp")
    copy_index = owner_index % copies
    tok_rows = tokens.shape[0]
    shard_width = w_gate.shape[0]
    capacity = max(2, 5 * tok_rows // (2 * experts))
    buckets = experts * capacity
    near = experts <= 8
    keys = expert_ids
    if near:
        keys = expert_ids ^ owner_index
        keys = (keys & 1) * 4 + (keys >> 1)

    lanes = jnp.arange(experts, dtype=jnp.int32)[None, :]
    first = keys[:, :1] == lanes
    second = keys[:, 1:] == lanes
    named = (first | second).astype(BF)
    earlier = (
        jnp.arange(tok_rows, dtype=jnp.int32)[None, :] < jnp.arange(tok_rows, dtype=jnp.int32)[:, None]
    ).astype(BF)
    before = jnp.dot(earlier, named, preferred_element_type=F32)
    slots = jnp.arange(buckets, dtype=jnp.int32)[None, :]

    def place(chosen, key):
        rank = jnp.sum(jnp.where(chosen, before, 0.0), axis=1, keepdims=True).astype(jnp.int32)
        return (slots == key * capacity + rank).astype(BF)

    place_0 = place(first, keys[:, :1])
    place_1 = place(second, keys[:, 1:])
    send_rows = lax.dot_general(
        place_0 + place_1, tokens, CONTRACT_ROWS, preferred_element_type=F32
    ).astype(BF)
    grad_f32 = out_grad.astype(F32)
    cot_0 = (route_weights[:, :1] * grad_f32).astype(BF)
    cot_1 = (route_weights[:, 1:] * grad_f32).astype(BF)
    cot_send = (
        lax.dot_general(place_0, cot_0, CONTRACT_ROWS, preferred_element_type=F32)
        + lax.dot_general(place_1, cot_1, CONTRACT_ROWS, preferred_element_type=F32)
    ).astype(BF)
    if near:
        in_rows = to_chips(*pair_core(send_rows))
        cot_send, in_rows[1] = after((by_chip(cot_send), in_rows[1]))
        cot_next = swap(cot_send[1], "expert", 2)
    else:
        in_rows = jnp.split(all_to_all(send_rows, experts), 2, axis=0)
        cot_rows = [all_to_all(cot_send, experts)]
    pieces = (w_gate, w_up, w_down)
    for bit_index in range(levels):
        partner = from_partner(as_sent(pieces), "expert", bit_index)
        is_upper = owner_index // 2**bit_index % 2 == 1
        pieces = tuple(relay_join(own, their, is_upper, 0) for own, their in zip(pieces, partner))
    gate_w, up_w, down_w = pieces

    def partial_product(rows, weights):
        return lax.dot_general(rows, weights, CONTRACT_FEATS, preferred_element_type=F32).astype(BF)

    half = gate_w.shape[0] // 2
    n = buckets // 4
    middle = len(in_rows) // 2
    near_rows = reorder(jnp.concatenate(in_rows[:middle], axis=0), me, 4)
    near_parts = partial_product(near_rows, gate_w), partial_product(near_rows, up_w)
    near_parts, far_rows = after((near_parts, in_rows[middle:]))
    if near:
        cot_send, far_rows = after((cot_send, far_rows))
        cot_rows = [cot_send[0], cot_next, swap(cot_send[2], "expert", 4), swap(cot_send[3], "expert", 6)]
    far_rows = reorder(jnp.concatenate(far_rows, axis=0), me, 4)
    in_rows = join_halves(near_rows, far_rows)
    part_gate = join_halves(near_parts[0], partial_product(far_rows, gate_w))
    part_up = join_halves(near_parts[1], partial_product(far_rows, up_w))
    halves = scatter_half(part_gate, part_up)
    last = scatter_quarter(part_gate, part_up, *halves)
    cot_rows, zeros = after_start(cot_rows, halves[0][:n, :1] + halves[1][:n, :1])
    if near:
        cot_rows = core_last(cot_rows)
    cot_halves = jnp.split(jnp.concatenate(cot_rows, axis=0), 2, axis=0)
    cot_rows = join_halves(*(reorder(rows, me, 4) for rows in cot_halves))

    part_hidden = partial_product(cot_rows, down_w)
    last, late_zeros = after_start(last, part_hidden[:n, :1])
    gate_sum = sum_quarter(part_gate, halves[0], last[1])
    up_sum = sum_quarter(part_up, halves[1], last[0])
    active, slope_term = silu_parts(gate_sum)
    own_hidden = (active * up_sum).astype(BF)

    part_first, part_second = part_hidden[:, :half], part_hidden[:, half:]
    via, more_zeros = after_start(scatter_far(part_first, part_second), own_hidden[:, :1])
    to_x, to_y = scatter_add(part_first, part_second, *via)
    own_hidden = (own_hidden[:, :half], own_hidden[:, half:])
    near_hidden = gather_near(*own_hidden)
    hidden = jnp.concatenate(gather_far(*own_hidden, *near_hidden), axis=1)
    grad_hidden = jnp.concatenate(scatter_near(part_first, part_second, to_x, to_y), axis=1) + zeros + late_zeros + more_zeros
    out_rows = jnp.dot(hidden, down_w, preferred_element_type=F32).astype(BF)

    own_grads = ((grad_hidden * up_sum * slope_term).astype(BF), (grad_hidden * active).astype(BF))
    hidden, near_grads = after((hidden, gather_near(*own_grads)))
    grad_rows = gather_far(*own_grads, *near_grads)
    back = jnp.concatenate([reorder(rows, me, 4) for rows in split_halves(out_rows)], axis=0)
    if near:
        back, grad_rows = after((from_chips(back), grad_rows))
        returned = from_core(back)
    else:
        returned = all_to_all(back, experts)
    weighted = (route_weights[:, :1] * place_0 + route_weights[:, 1:] * place_1).astype(BF)
    output = jnp.dot(weighted, returned, preferred_element_type=F32).astype(BF)

    def term(left, right):
        return lax.dot_general(left, right, CONTRACT_ROWS, preferred_element_type=F32).astype(BF)

    grad_terms = (term(grad_rows[0], in_rows), term(grad_rows[1], in_rows), term(hidden, cot_rows))
    for bit_index in range(levels):
        partner = from_partner(grad_terms, "expert", bit_index)
        grad_terms = tuple(add_round(own, their) for own, their in zip(grad_terms, partner))
    start_row = copy_index * shard_width
    grads = [lax.dynamic_slice_in_dim(each, start_row, shard_width, 0) for each in grad_terms]
    return (output, *grads)


def solution(mesh):
    split = P("expert", "dp")
    pairs = P("expert", None)
    return jax.shard_map(
        per_device,
        mesh=mesh,
        in_specs=(split, pairs, pairs, split, split, split, split),
        out_specs=(split, split, split, split),
        check_vma=False,
    )
```

```python
import jax
import jax.numpy as jnp
from jax import lax
from jax.experimental import pallas as pl
from jax.experimental.pallas import tpu as pltpu
from jax.sharding import PartitionSpec as P

BF = jnp.bfloat16
F32 = jnp.float32


def as_sent(array):

    def short(part):
        return part.astype(BF) if part.dtype == F32 else part

    return jax.tree.map(short, array)


def from_partner(block, axis, bit):
    count = lax.axis_size(axis)
    route = []
    for low in range(count):
        high = low | 1 << bit
        if high != low and high < count:
            route += [(low, high), (high, low)]
    return lax.ppermute(block, axis, route)


def swap(block, axis, mask):
    count = lax.axis_size(axis)
    return lax.ppermute(block, axis, [(i, i ^ mask) for i in range(count)])


def after(values):
    return lax.optimization_barrier(values)


def after_start(value, earlier):
    value, column = after((value, earlier))
    return value, 0.0 * column.astype(F32)


def silu_parts(gate_sum):
    gate_sigmoid = jax.nn.sigmoid(gate_sum)
    return (gate_sum * gate_sigmoid, gate_sigmoid * (1.0 + gate_sum * (1.0 - gate_sigmoid)))


def relay_join(own_part, their_part, is_upper, join_axis):
    lower_first = jnp.concatenate([own_part, their_part], axis=join_axis)
    upper_first = jnp.concatenate([their_part, own_part], axis=join_axis)
    return jnp.where(is_upper, upper_first, lower_first)


def add_round(own_part, their_part):
    return (own_part.astype(F32) + their_part.astype(F32)).astype(BF)


def reorder(rows, key, parts):
    blocks = rows.reshape(parts, rows.shape[0] // parts, rows.shape[1])
    return jnp.concatenate(
        [lax.dynamic_index_in_dim(blocks, key ^ i, 0, keepdims=False) for i in range(parts)], axis=0
    )


def all_to_all(rows, experts):
    moved = lax.all_to_all(
        rows.reshape(experts, rows.shape[0] // experts, rows.shape[1]),
        "expert",
        split_axis=0,
        concat_axis=0,
        tiled=True,
    )
    return moved.reshape(rows.shape)


def pair_core(rows):
    n = rows.shape[0] // 2
    return rows[:n], swap(rows[n:], "expert", 1)


def to_chips(own, other):
    n = own.shape[0] // 4
    blocks = [
        jnp.concatenate([own[m * n:(m + 1) * n], other[m * n:(m + 1) * n]], axis=0) for m in range(4)
    ]
    return [blocks[0]] + [swap(blocks[m], "expert", 2 * m) for m in range(1, 4)]


def to_chips_first(rows):
    n = rows.shape[0] // 8
    blocks = [
        jnp.concatenate([rows[m * n:(m + 1) * n], rows[(4 + m) * n:(5 + m) * n]], axis=0) for m in range(4)
    ]
    return [blocks[0]] + [swap(blocks[m], "expert", 2 * m) for m in range(1, 4)]


def core_last(got):
    n = got[0].shape[0] // 2
    other = swap(jnp.concatenate([each[n:] for each in got], axis=0), "expert", 1)
    rows = []
    for m, each in enumerate(got):
        rows += [each[:n], other[m * n:(m + 1) * n]]
    return rows


def from_chips(rows):
    n = rows.shape[0] // 4
    return [rows[:n]] + [swap(rows[m * n:(m + 1) * n], "expert", 2 * m) for m in range(1, 4)]


def from_core(back):
    n = back[0].shape[0] // 2
    other = swap(jnp.concatenate([each[n:] for each in back], axis=0), "expert", 1)
    return jnp.concatenate([each[:n] for each in back] + [other], axis=0)


def scatter_far(first, second):
    n = first.shape[0] // 4
    return swap(first[3 * n:], "dp", 1), swap(second[3 * n:], "dp", 2)


def scatter_add(first, second, via_x, via_y):
    n = first.shape[0] // 4
    to_x = jnp.concatenate([first[n:2 * n], add_round(second[n:2 * n], via_y)], axis=1)
    to_y = jnp.concatenate([add_round(first[2 * n:3 * n], via_x), second[2 * n:3 * n]], axis=1)
    return to_x, to_y


def scatter_near(first, second, to_x, to_y):
    n = first.shape[0] // 4
    c = first.shape[1]
    from_x = swap(to_x, "dp", 1)
    from_y = swap(to_y, "dp", 2)
    return tuple(
        own[:n].astype(F32) + x.astype(F32) + y.astype(F32)
        for own, x, y in ((first, from_x[:, :c], from_y[:, :c]), (second, from_x[:, c:], from_y[:, c:]))
    )


def gather_near(first, second):
    own = jnp.concatenate([first, second], axis=1)
    return swap(own, "dp", 1), swap(own, "dp", 2)


def gather_far(first, second, from_x, from_y):
    c = first.shape[1]
    far_first = swap(from_y[:, :c], "dp", 1)
    far_second = swap(from_x[:, c:], "dp", 2)
    return (
        jnp.concatenate([first, from_x[:, :c], from_y[:, :c], far_first], axis=0),
        jnp.concatenate([second, from_x[:, c:], from_y[:, c:], far_second], axis=0),
    )


CONTRACT_FEATS = (((1,), (1,)), ((), ()))
CONTRACT_ROWS = (((0,), (0,)), ((), ()))


def two_terms(first, second, rows):
    count, width = first.shape
    feats = rows.shape[1]
    block = 256

    def kernel(first_ref, second_ref, rows_ref, first_out, second_out):
        lines = lax.broadcasted_iota(jnp.int32, (block, block), 0)
        identity = (lines == lax.broadcasted_iota(jnp.int32, (block, block), 1)).astype(BF)
        for left_ref, out in ((first_ref, first_out), (second_ref, second_out)):
            turned = lax.dot_general(identity, left_ref[...], CONTRACT_FEATS, preferred_element_type=F32)
            out[...] = jnp.dot(turned.astype(BF), rows_ref[...], preferred_element_type=F32).astype(BF)

    left_spec = pl.BlockSpec((count, block), lambda i: (0, i))
    out_spec = pl.BlockSpec((block, feats), lambda i: (i, 0))
    out = jax.ShapeDtypeStruct((width, feats), BF)
    return pl.pallas_call(
        kernel,
        grid=(width // block,),
        in_specs=[left_spec, left_spec, pl.BlockSpec((count, feats), lambda i: (0, 0))],
        out_specs=[out_spec, out_spec],
        out_shape=[out, out],
        compiler_params=pltpu.CompilerParams(vmem_limit_bytes=24 * 2**20),
        cost_estimate=pl.CostEstimate(
            flops=16 * count * width * feats,
            bytes_accessed=16 * (count + feats) * width,
            transcendentals=0,
        ),
    )(first, second, rows)


def per_device(tokens, expert_ids, route_weights, w_gate, w_up, w_down, out_grad):
    experts = lax.axis_size("expert")
    copies = experts // 8
    levels = copies.bit_length() - 1
    owner_index = lax.axis_index("expert")
    me = lax.axis_index("dp")
    copy_index = owner_index % copies
    tok_rows = tokens.shape[0]
    shard_width = w_gate.shape[0]
    capacity = max(2, 5 * tok_rows // (2 * experts))
    buckets = experts * capacity
    near = experts <= 8
    keys = expert_ids
    if near:
        keys = expert_ids ^ owner_index
        keys = (keys & 1) * 4 + (keys >> 1)

    lanes = jnp.arange(experts, dtype=jnp.int32)[None, :]
    first = keys[:, :1] == lanes
    second = keys[:, 1:] == lanes
    named = (first | second).astype(BF)
    earlier = (
        jnp.arange(tok_rows, dtype=jnp.int32)[None, :] < jnp.arange(tok_rows, dtype=jnp.int32)[:, None]
    ).astype(BF)
    before = jnp.dot(earlier, named, preferred_element_type=F32)
    slots = jnp.arange(buckets, dtype=jnp.int32)[None, :]

    def place(chosen, key):
        rank = jnp.sum(jnp.where(chosen, before, 0.0), axis=1, keepdims=True).astype(jnp.int32)
        return (slots == key * capacity + rank).astype(BF)

    place_0 = place(first, keys[:, :1])
    place_1 = place(second, keys[:, 1:])
    send_rows = lax.dot_general(
        place_0 + place_1, tokens, CONTRACT_ROWS, preferred_element_type=F32
    ).astype(BF)
    grad_f32 = out_grad.astype(F32)
    cot_0 = (route_weights[:, :1] * grad_f32).astype(BF)
    cot_1 = (route_weights[:, 1:] * grad_f32).astype(BF)
    cot_send = (
        lax.dot_general(place_0, cot_0, CONTRACT_ROWS, preferred_element_type=F32)
        + lax.dot_general(place_1, cot_1, CONTRACT_ROWS, preferred_element_type=F32)
    ).astype(BF)
    if near:
        in_rows = to_chips(*pair_core(send_rows))
        cot_send, in_rows = after((cot_send, in_rows))
        cot_rows = to_chips_first(cot_send)
    else:
        in_rows = [all_to_all(send_rows, experts)]
        cot_rows = [all_to_all(cot_send, experts)]
    in_rows = reorder(jnp.concatenate(in_rows, axis=0), me, 4)

    pieces = (w_gate, w_up, w_down)
    for bit_index in range(levels):
        partner = from_partner(as_sent(pieces), "expert", bit_index)
        is_upper = owner_index // 2**bit_index % 2 == 1
        pieces = tuple(relay_join(own, their, is_upper, 0) for own, their in zip(pieces, partner))
    gate_w, up_w, down_w = pieces

    def partial_product(rows, weights):
        return lax.dot_general(rows, weights, CONTRACT_FEATS, preferred_element_type=F32).astype(BF)

    half = gate_w.shape[0] // 2
    part_gate, part_up = partial_product(in_rows, gate_w), partial_product(in_rows, up_w)
    to_x, to_y = scatter_add(part_gate, part_up, *scatter_far(part_gate, part_up))
    gate_sum, up_sum = scatter_near(part_gate, part_up, to_x, to_y)
    cot_rows, zeros = after_start(cot_rows, to_x[:, -1:] + to_y[:, :1])
    if near:
        cot_rows = core_last(cot_rows)
    cot_rows = reorder(jnp.concatenate(cot_rows, axis=0), me, 4)

    active, slope_term = silu_parts(gate_sum)
    own_hidden = (active * up_sum).astype(BF)

    part_hidden = partial_product(cot_rows, down_w)
    part_first, part_second = part_hidden[:, :half], part_hidden[:, half:]
    via, more_zeros = after_start(scatter_far(part_first, part_second), own_hidden[:, :1])
    to_x, to_y = scatter_add(part_first, part_second, *via)
    own_hidden = (own_hidden[:, :half], own_hidden[:, half:])
    near_hidden = gather_near(*own_hidden)
    hidden = jnp.concatenate(gather_far(*own_hidden, *near_hidden), axis=1)
    grad_hidden = jnp.concatenate(scatter_near(part_first, part_second, to_x, to_y), axis=1) + zeros + more_zeros
    out_rows = jnp.dot(hidden, down_w, preferred_element_type=F32).astype(BF)

    own_grads = ((grad_hidden * up_sum * slope_term).astype(BF), (grad_hidden * active).astype(BF))
    hidden, near_grads = after((hidden, gather_near(*own_grads)))
    grad_rows = gather_far(*own_grads, *near_grads)
    back = reorder(out_rows, me, 4)
    if near:
        back, grad_rows = after((from_chips(back), grad_rows))
        returned = from_core(back)
    else:
        returned = all_to_all(back, experts)
    weighted = (route_weights[:, :1] * place_0 + route_weights[:, 1:] * place_1).astype(BF)
    output = jnp.dot(weighted, returned, preferred_element_type=F32).astype(BF)

    def term(left, right):
        return lax.dot_general(left, right, CONTRACT_ROWS, preferred_element_type=F32).astype(BF)

    down_term, grad_rows = after((term(hidden, cot_rows), grad_rows))
    grad_terms = (*two_terms(*grad_rows, in_rows), down_term)
    for bit_index in range(levels):
        partner = from_partner(grad_terms, "expert", bit_index)
        grad_terms = tuple(add_round(own, their) for own, their in zip(grad_terms, partner))
    start_row = copy_index * shard_width
    grads = [lax.dynamic_slice_in_dim(each, start_row, shard_width, 0) for each in grad_terms]
    return (output, *grads)


def solution(mesh):
    split = P("expert", "dp")
    pairs = P("expert", None)
    return jax.shard_map(
        per_device,
        mesh=mesh,
        in_specs=(split, pairs, pairs, split, split, split, split),
        out_specs=(split, split, split, split),
        check_vma=False,
    )
```

```python
import jax
import jax.numpy as jnp
from jax import lax
from jax.experimental import pallas as pl
from jax.experimental.pallas import tpu as pltpu
from jax.sharding import PartitionSpec as P

BF = jnp.bfloat16
F32 = jnp.float32


def as_sent(array):

    def short(part):
        return part.astype(BF) if part.dtype == F32 else part

    return jax.tree.map(short, array)


def from_partner(block, axis, bit):
    count = lax.axis_size(axis)
    route = []
    for low in range(count):
        high = low | 1 << bit
        if high != low and high < count:
            route += [(low, high), (high, low)]
    return lax.ppermute(block, axis, route)


def swap(block, axis, mask):
    count = lax.axis_size(axis)
    return lax.ppermute(block, axis, [(i, i ^ mask) for i in range(count)])


def after(values):
    return lax.optimization_barrier(values)


def after_start(value, earlier):
    value, column = after((value, earlier))
    return value, 0.0 * column.astype(F32)


def silu_parts(gate_sum):
    gate_sigmoid = jax.nn.sigmoid(gate_sum)
    return (gate_sum * gate_sigmoid, gate_sigmoid * (1.0 + gate_sum * (1.0 - gate_sigmoid)))


def relay_join(own_part, their_part, is_upper, join_axis):
    lower_first = jnp.concatenate([own_part, their_part], axis=join_axis)
    upper_first = jnp.concatenate([their_part, own_part], axis=join_axis)
    return jnp.where(is_upper, upper_first, lower_first)


def add_round(own_part, their_part):
    return (own_part.astype(F32) + their_part.astype(F32)).astype(BF)


def reorder(rows, key, parts):
    blocks = rows.reshape(parts, rows.shape[0] // parts, rows.shape[1])
    return jnp.concatenate(
        [lax.dynamic_index_in_dim(blocks, key ^ i, 0, keepdims=False) for i in range(parts)], axis=0
    )


def all_to_all(rows, experts):
    moved = lax.all_to_all(
        rows.reshape(experts, rows.shape[0] // experts, rows.shape[1]),
        "expert",
        split_axis=0,
        concat_axis=0,
        tiled=True,
    )
    return moved.reshape(rows.shape)


def pair_core(rows):
    n = rows.shape[0] // 2
    return rows[:n], swap(rows[n:], "expert", 1)


def to_chips(own, other):
    n = own.shape[0] // 4
    blocks = [
        jnp.concatenate([own[m * n:(m + 1) * n], other[m * n:(m + 1) * n]], axis=0) for m in range(4)
    ]
    return [blocks[0]] + [swap(blocks[m], "expert", 2 * m) for m in range(1, 4)]


def to_chips_first(rows):
    n = rows.shape[0] // 8
    blocks = [
        jnp.concatenate([rows[m * n:(m + 1) * n], rows[(4 + m) * n:(5 + m) * n]], axis=0) for m in range(4)
    ]
    return [blocks[0]] + [swap(blocks[m], "expert", 2 * m) for m in range(1, 4)]


def core_last(got):
    n = got[0].shape[0] // 2
    other = swap(jnp.concatenate([each[n:] for each in got], axis=0), "expert", 1)
    rows = []
    for m, each in enumerate(got):
        rows += [each[:n], other[m * n:(m + 1) * n]]
    return rows


def from_chips(rows):
    n = rows.shape[0] // 4
    return [rows[:n]] + [swap(rows[m * n:(m + 1) * n], "expert", 2 * m) for m in range(1, 4)]


def from_core(back):
    n = back[0].shape[0] // 2
    other = swap(jnp.concatenate([each[n:] for each in back], axis=0), "expert", 1)
    return jnp.concatenate([each[:n] for each in back] + [other], axis=0)


def scatter_far(first, second):
    n = first.shape[0] // 4
    return swap(first[3 * n:], "dp", 1), swap(second[3 * n:], "dp", 2)


def scatter_add(first, second, via_x, via_y):
    n = first.shape[0] // 4
    to_x = jnp.concatenate([first[n:2 * n], add_round(second[n:2 * n], via_y)], axis=1)
    to_y = jnp.concatenate([add_round(first[2 * n:3 * n], via_x), second[2 * n:3 * n]], axis=1)
    return to_x, to_y


def scatter_near(first, second, to_x, to_y):
    n = first.shape[0] // 4
    c = first.shape[1]
    from_x = swap(to_x, "dp", 1)
    from_y = swap(to_y, "dp", 2)
    return tuple(
        own[:n].astype(F32) + x.astype(F32) + y.astype(F32)
        for own, x, y in ((first, from_x[:, :c], from_y[:, :c]), (second, from_x[:, c:], from_y[:, c:]))
    )


def gather_near(first, second):
    own = jnp.concatenate([first, second], axis=1)
    return swap(own, "dp", 1), swap(own, "dp", 2)


def gather_far(first, second, from_x, from_y):
    c = first.shape[1]
    far_first = swap(from_y[:, :c], "dp", 1)
    far_second = swap(from_x[:, c:], "dp", 2)
    return (
        jnp.concatenate([first, from_x[:, :c], from_y[:, :c], far_first], axis=0),
        jnp.concatenate([second, from_x[:, c:], from_y[:, c:], far_second], axis=0),
    )


CONTRACT_FEATS = (((1,), (1,)), ((), ()))
CONTRACT_ROWS = (((0,), (0,)), ((), ()))


def two_terms(first, second, rows):
    count, width = first.shape
    feats = rows.shape[1]
    block = width // 2

    def kernel(first_ref, second_ref, rows_ref, first_out, second_out):
        for left_ref, out in ((first_ref, first_out), (second_ref, second_out)):
            out[...] = lax.dot_general(
                left_ref[...], rows_ref[...], CONTRACT_ROWS, preferred_element_type=F32
            ).astype(BF)

    left_spec = pl.BlockSpec((count, block), lambda i: (0, i))
    out_spec = pl.BlockSpec((block, feats), lambda i: (i, 0))
    out = jax.ShapeDtypeStruct((width, feats), BF)
    return pl.pallas_call(
        kernel,
        grid=(width // block,),
        in_specs=[left_spec, left_spec, pl.BlockSpec((count, feats), lambda i: (0, 0))],
        out_specs=[out_spec, out_spec],
        out_shape=[out, out],
        compiler_params=pltpu.CompilerParams(vmem_limit_bytes=36 * 2**20),
        cost_estimate=pl.CostEstimate(
            flops=16 * count * width * feats,
            bytes_accessed=16 * (count + feats) * width,
            transcendentals=0,
        ),
    )(first, second, rows)


def per_device(tokens, expert_ids, route_weights, w_gate, w_up, w_down, out_grad):
    experts = lax.axis_size("expert")
    copies = experts // 8
    levels = copies.bit_length() - 1
    owner_index = lax.axis_index("expert")
    me = lax.axis_index("dp")
    copy_index = owner_index % copies
    tok_rows = tokens.shape[0]
    shard_width = w_gate.shape[0]
    capacity = max(2, 5 * tok_rows // (2 * experts))
    buckets = experts * capacity
    near = experts <= 8
    keys = expert_ids
    if near:
        keys = expert_ids ^ owner_index
        keys = (keys & 1) * 4 + (keys >> 1)

    lanes = jnp.arange(experts, dtype=jnp.int32)[None, :]
    first = keys[:, :1] == lanes
    second = keys[:, 1:] == lanes
    named = (first | second).astype(BF)
    earlier = (
        jnp.arange(tok_rows, dtype=jnp.int32)[None, :] < jnp.arange(tok_rows, dtype=jnp.int32)[:, None]
    ).astype(BF)
    before = jnp.dot(earlier, named, preferred_element_type=F32)
    slots = jnp.arange(buckets, dtype=jnp.int32)[None, :]

    def place(chosen, key):
        rank = jnp.sum(jnp.where(chosen, before, 0.0), axis=1, keepdims=True).astype(jnp.int32)
        return (slots == key * capacity + rank).astype(BF)

    place_0 = place(first, keys[:, :1])
    place_1 = place(second, keys[:, 1:])
    send_rows = lax.dot_general(
        place_0 + place_1, tokens, CONTRACT_ROWS, preferred_element_type=F32
    ).astype(BF)
    grad_f32 = out_grad.astype(F32)
    cot_0 = (route_weights[:, :1] * grad_f32).astype(BF)
    cot_1 = (route_weights[:, 1:] * grad_f32).astype(BF)
    cot_send = (
        lax.dot_general(place_0, cot_0, CONTRACT_ROWS, preferred_element_type=F32)
        + lax.dot_general(place_1, cot_1, CONTRACT_ROWS, preferred_element_type=F32)
    ).astype(BF)
    if near:
        in_rows = to_chips(*pair_core(send_rows))
        cot_send, in_rows = after((cot_send, in_rows))
        cot_rows = to_chips_first(cot_send)
    else:
        in_rows = [all_to_all(send_rows, experts)]
        cot_rows = [all_to_all(cot_send, experts)]
    in_rows = reorder(jnp.concatenate(in_rows, axis=0), me, 4)

    pieces = (w_gate, w_up, w_down)
    for bit_index in range(levels):
        partner = from_partner(as_sent(pieces), "expert", bit_index)
        is_upper = owner_index // 2**bit_index % 2 == 1
        pieces = tuple(relay_join(own, their, is_upper, 0) for own, their in zip(pieces, partner))
    gate_w, up_w, down_w = pieces

    def partial_product(rows, weights):
        return lax.dot_general(rows, weights, CONTRACT_FEATS, preferred_element_type=F32).astype(BF)

    half = gate_w.shape[0] // 2
    part_gate, part_up = partial_product(in_rows, gate_w), partial_product(in_rows, up_w)
    to_x, to_y = scatter_add(part_gate, part_up, *scatter_far(part_gate, part_up))
    gate_sum, up_sum = scatter_near(part_gate, part_up, to_x, to_y)
    cot_rows, zeros = after_start(cot_rows, to_x[:, -1:] + to_y[:, :1])
    if near:
        cot_rows = core_last(cot_rows)
    cot_rows = reorder(jnp.concatenate(cot_rows, axis=0), me, 4)

    active, slope_term = silu_parts(gate_sum)
    own_hidden = (active * up_sum).astype(BF)

    part_hidden = partial_product(cot_rows, down_w)
    part_first, part_second = part_hidden[:, :half], part_hidden[:, half:]
    via, more_zeros = after_start(scatter_far(part_first, part_second), own_hidden[:, :1])
    to_x, to_y = scatter_add(part_first, part_second, *via)
    own_hidden = (own_hidden[:, :half], own_hidden[:, half:])
    near_hidden = gather_near(*own_hidden)
    hidden = jnp.concatenate(gather_far(*own_hidden, *near_hidden), axis=1)
    grad_hidden = jnp.concatenate(scatter_near(part_first, part_second, to_x, to_y), axis=1) + zeros + more_zeros
    out_rows = jnp.dot(hidden, down_w, preferred_element_type=F32).astype(BF)

    own_grads = ((grad_hidden * up_sum * slope_term).astype(BF), (grad_hidden * active).astype(BF))
    hidden, near_grads = after((hidden, gather_near(*own_grads)))
    grad_rows = gather_far(*own_grads, *near_grads)
    back = reorder(out_rows, me, 4)
    if near:
        back, grad_rows = after((from_chips(back), grad_rows))
        returned = from_core(back)
    else:
        returned = all_to_all(back, experts)
    weighted = (route_weights[:, :1] * place_0 + route_weights[:, 1:] * place_1).astype(BF)
    output = jnp.dot(weighted, returned, preferred_element_type=F32).astype(BF)

    def term(left, right):
        return lax.dot_general(left, right, CONTRACT_ROWS, preferred_element_type=F32).astype(BF)

    down_term, grad_rows = after((term(hidden, cot_rows), grad_rows))
    grad_terms = (*two_terms(*grad_rows, in_rows), down_term)
    for bit_index in range(levels):
        partner = from_partner(grad_terms, "expert", bit_index)
        grad_terms = tuple(add_round(own, their) for own, their in zip(grad_terms, partner))
    start_row = copy_index * shard_width
    grads = [lax.dynamic_slice_in_dim(each, start_row, shard_width, 0) for each in grad_terms]
    return (output, *grads)


def solution(mesh):
    split = P("expert", "dp")
    pairs = P("expert", None)
    return jax.shard_map(
        per_device,
        mesh=mesh,
        in_specs=(split, pairs, pairs, split, split, split, split),
        out_specs=(split, split, split, split),
        check_vma=False,
    )
```

```python
import jax
import jax.numpy as jnp
from jax import lax
from jax.experimental import pallas as pl
from jax.experimental.pallas import tpu as pltpu
from jax.sharding import PartitionSpec as P

BF = jnp.bfloat16
F32 = jnp.float32


def as_sent(array):

    def short(part):
        return part.astype(BF) if part.dtype == F32 else part

    return jax.tree.map(short, array)


def from_partner(block, axis, bit):
    count = lax.axis_size(axis)
    route = []
    for low in range(count):
        high = low | 1 << bit
        if high != low and high < count:
            route += [(low, high), (high, low)]
    return lax.ppermute(block, axis, route)


def swap(block, axis, mask):
    count = lax.axis_size(axis)
    return lax.ppermute(block, axis, [(i, i ^ mask) for i in range(count)])


def after(values):
    return lax.optimization_barrier(values)


def after_start(value, earlier):
    value, column = after((value, earlier))
    return value, 0.0 * column.astype(F32)


def silu_parts(gate_sum):
    gate_sigmoid = jax.nn.sigmoid(gate_sum)
    return (gate_sum * gate_sigmoid, gate_sigmoid * (1.0 + gate_sum * (1.0 - gate_sigmoid)))


def relay_join(own_part, their_part, is_upper, join_axis):
    lower_first = jnp.concatenate([own_part, their_part], axis=join_axis)
    upper_first = jnp.concatenate([their_part, own_part], axis=join_axis)
    return jnp.where(is_upper, upper_first, lower_first)


def add_round(own_part, their_part):
    return (own_part.astype(F32) + their_part.astype(F32)).astype(BF)


def reorder(rows, key, parts):
    blocks = rows.reshape(parts, rows.shape[0] // parts, rows.shape[1])
    return jnp.concatenate(
        [lax.dynamic_index_in_dim(blocks, key ^ i, 0, keepdims=False) for i in range(parts)], axis=0
    )


def all_to_all(rows, experts):
    moved = lax.all_to_all(
        rows.reshape(experts, rows.shape[0] // experts, rows.shape[1]),
        "expert",
        split_axis=0,
        concat_axis=0,
        tiled=True,
    )
    return moved.reshape(rows.shape)


def pair_core(rows):
    n = rows.shape[0] // 2
    return rows[:n], swap(rows[n:], "expert", 1)


def to_chips(own, other):
    n = own.shape[0] // 4
    blocks = [
        jnp.concatenate([own[m * n:(m + 1) * n], other[m * n:(m + 1) * n]], axis=0) for m in range(4)
    ]
    return [blocks[0]] + [swap(blocks[m], "expert", 2 * m) for m in range(1, 4)]


def to_chips_first(rows):
    n = rows.shape[0] // 8
    blocks = [
        jnp.concatenate([rows[m * n:(m + 1) * n], rows[(4 + m) * n:(5 + m) * n]], axis=0) for m in range(4)
    ]
    return [blocks[0]] + [swap(blocks[m], "expert", 2 * m) for m in range(1, 4)]


def core_last(got):
    n = got[0].shape[0] // 2
    other = swap(jnp.concatenate([each[n:] for each in got], axis=0), "expert", 1)
    rows = []
    for m, each in enumerate(got):
        rows += [each[:n], other[m * n:(m + 1) * n]]
    return rows


def from_chips(rows):
    n = rows.shape[0] // 4
    return [rows[:n]] + [swap(rows[m * n:(m + 1) * n], "expert", 2 * m) for m in range(1, 4)]


def from_core(back):
    n = back[0].shape[0] // 2
    other = swap(jnp.concatenate([each[n:] for each in back], axis=0), "expert", 1)
    return jnp.concatenate([each[:n] for each in back] + [other], axis=0)


def scatter_far(first, second):
    n = first.shape[0] // 4
    return swap(first[3 * n:], "dp", 1), swap(second[3 * n:], "dp", 2)


def scatter_add(first, second, via_x, via_y):
    n = first.shape[0] // 4
    to_x = jnp.concatenate([first[n:2 * n], add_round(second[n:2 * n], via_y)], axis=1)
    to_y = jnp.concatenate([add_round(first[2 * n:3 * n], via_x), second[2 * n:3 * n]], axis=1)
    return to_x, to_y


def scatter_near(first, second, to_x, to_y):
    n = first.shape[0] // 4
    c = first.shape[1]
    from_x = swap(to_x, "dp", 1)
    from_y = swap(to_y, "dp", 2)
    return tuple(
        own[:n].astype(F32) + x.astype(F32) + y.astype(F32)
        for own, x, y in ((first, from_x[:, :c], from_y[:, :c]), (second, from_x[:, c:], from_y[:, c:]))
    )


def gather_near(first, second):
    own = jnp.concatenate([first, second], axis=1)
    return swap(own, "dp", 1), swap(own, "dp", 2)


def gather_far(first, second, from_x, from_y):
    c = first.shape[1]
    far_first = swap(from_y[:, :c], "dp", 1)
    far_second = swap(from_x[:, c:], "dp", 2)
    return (
        jnp.concatenate([first, from_x[:, :c], from_y[:, :c], far_first], axis=0),
        jnp.concatenate([second, from_x[:, c:], from_y[:, c:], far_second], axis=0),
    )


CONTRACT_FEATS = (((1,), (1,)), ((), ()))
CONTRACT_ROWS = (((0,), (0,)), ((), ()))


def two_terms(first, second, rows):
    count, width = first.shape
    feats = rows.shape[1]
    cuts = ((0, width // 2, width), (0, width // 2, width - 256, width))

    def kernel(first_ref, second_ref, rows_ref, first_out, second_out, first_held, second_held, sems):
        copies = []
        refs = ((first_ref, first_out, first_held), (second_ref, second_out, second_held))
        for (left_ref, out, held), ends in zip(refs, cuts):
            for low, high in zip(ends, ends[1:]):
                held[low:high, :] = lax.dot_general(
                    left_ref[:, low:high], rows_ref[...], CONTRACT_ROWS, preferred_element_type=F32
                ).astype(BF)
                copy = pltpu.make_async_copy(held.at[low:high], out.at[low:high], sems.at[len(copies)])
                copy.start()
                copies.append(copy)
        for copy in copies:
            copy.wait()

    whole = pl.BlockSpec(memory_space=pltpu.VMEM)
    anywhere = pl.BlockSpec(memory_space=pl.ANY)
    out = jax.ShapeDtypeStruct((width, feats), BF)
    return pl.pallas_call(
        kernel,
        in_specs=[whole, whole, whole],
        out_specs=[anywhere, anywhere],
        out_shape=[out, out],
        scratch_shapes=[
            pltpu.VMEM((width, feats), BF),
            pltpu.VMEM((width, feats), BF),
            pltpu.SemaphoreType.DMA((5,)),
        ],
        compiler_params=pltpu.CompilerParams(vmem_limit_bytes=36 * 2**20),
        cost_estimate=pl.CostEstimate(
            flops=16 * count * width * feats,
            bytes_accessed=16 * (count + feats) * width,
            transcendentals=0,
        ),
    )(first, second, rows)


def per_device(tokens, expert_ids, route_weights, w_gate, w_up, w_down, out_grad):
    experts = lax.axis_size("expert")
    copies = experts // 8
    levels = copies.bit_length() - 1
    owner_index = lax.axis_index("expert")
    me = lax.axis_index("dp")
    copy_index = owner_index % copies
    tok_rows = tokens.shape[0]
    shard_width = w_gate.shape[0]
    capacity = max(2, 5 * tok_rows // (2 * experts))
    buckets = experts * capacity
    near = experts <= 8
    keys = expert_ids
    if near:
        keys = expert_ids ^ owner_index
        keys = (keys & 1) * 4 + (keys >> 1)

    lanes = jnp.arange(experts, dtype=jnp.int32)[None, :]
    first = keys[:, :1] == lanes
    second = keys[:, 1:] == lanes
    named = (first | second).astype(BF)
    earlier = (
        jnp.arange(tok_rows, dtype=jnp.int32)[None, :] < jnp.arange(tok_rows, dtype=jnp.int32)[:, None]
    ).astype(BF)
    before = jnp.dot(earlier, named, preferred_element_type=F32)
    slots = jnp.arange(buckets, dtype=jnp.int32)[None, :]

    def place(chosen, key):
        rank = jnp.sum(jnp.where(chosen, before, 0.0), axis=1, keepdims=True).astype(jnp.int32)
        return (slots == key * capacity + rank).astype(BF)

    place_0 = place(first, keys[:, :1])
    place_1 = place(second, keys[:, 1:])
    send_rows = lax.dot_general(
        place_0 + place_1, tokens, CONTRACT_ROWS, preferred_element_type=F32
    ).astype(BF)
    grad_f32 = out_grad.astype(F32)
    cot_0 = (route_weights[:, :1] * grad_f32).astype(BF)
    cot_1 = (route_weights[:, 1:] * grad_f32).astype(BF)
    cot_send = (
        lax.dot_general(place_0, cot_0, CONTRACT_ROWS, preferred_element_type=F32)
        + lax.dot_general(place_1, cot_1, CONTRACT_ROWS, preferred_element_type=F32)
    ).astype(BF)
    if near:
        in_rows = to_chips(*pair_core(send_rows))
        cot_send, in_rows = after((cot_send, in_rows))
        cot_rows = to_chips_first(cot_send)
    else:
        in_rows = [all_to_all(send_rows, experts)]
        cot_rows = [all_to_all(cot_send, experts)]
    in_rows = reorder(jnp.concatenate(in_rows, axis=0), me, 4)

    pieces = (w_gate, w_up, w_down)
    for bit_index in range(levels):
        partner = from_partner(as_sent(pieces), "expert", bit_index)
        is_upper = owner_index // 2**bit_index % 2 == 1
        pieces = tuple(relay_join(own, their, is_upper, 0) for own, their in zip(pieces, partner))
    gate_w, up_w, down_w = pieces

    def partial_product(rows, weights):
        return lax.dot_general(rows, weights, CONTRACT_FEATS, preferred_element_type=F32).astype(BF)

    half = gate_w.shape[0] // 2
    part_gate, part_up = partial_product(in_rows, gate_w), partial_product(in_rows, up_w)
    to_x, to_y = scatter_add(part_gate, part_up, *scatter_far(part_gate, part_up))
    gate_sum, up_sum = scatter_near(part_gate, part_up, to_x, to_y)
    cot_rows, zeros = after_start(cot_rows, to_x[:, -1:] + to_y[:, :1])
    if near:
        cot_rows = core_last(cot_rows)
    cot_rows = reorder(jnp.concatenate(cot_rows, axis=0), me, 4)

    active, slope_term = silu_parts(gate_sum)
    own_hidden = (active * up_sum).astype(BF)

    part_hidden = partial_product(cot_rows, down_w)
    part_first, part_second = part_hidden[:, :half], part_hidden[:, half:]
    via, more_zeros = after_start(scatter_far(part_first, part_second), own_hidden[:, :1])
    to_x, to_y = scatter_add(part_first, part_second, *via)
    own_hidden = (own_hidden[:, :half], own_hidden[:, half:])
    near_hidden = gather_near(*own_hidden)
    hidden = jnp.concatenate(gather_far(*own_hidden, *near_hidden), axis=1)
    grad_hidden = jnp.concatenate(scatter_near(part_first, part_second, to_x, to_y), axis=1) + zeros + more_zeros
    out_rows = jnp.dot(hidden, down_w, preferred_element_type=F32).astype(BF)

    own_grads = ((grad_hidden * up_sum * slope_term).astype(BF), (grad_hidden * active).astype(BF))
    hidden, near_grads = after((hidden, gather_near(*own_grads)))
    grad_rows = gather_far(*own_grads, *near_grads)
    back = reorder(out_rows, me, 4)
    if near:
        back, grad_rows = after((from_chips(back), grad_rows))
        returned = from_core(back)
    else:
        returned = all_to_all(back, experts)
    weighted = (route_weights[:, :1] * place_0 + route_weights[:, 1:] * place_1).astype(BF)
    output = jnp.dot(weighted, returned, preferred_element_type=F32).astype(BF)

    def term(left, right):
        return lax.dot_general(left, right, CONTRACT_ROWS, preferred_element_type=F32).astype(BF)

    down_term, grad_rows = after((term(hidden, cot_rows), grad_rows))
    grad_terms = (*two_terms(*grad_rows, in_rows), down_term)
    for bit_index in range(levels):
        partner = from_partner(grad_terms, "expert", bit_index)
        grad_terms = tuple(add_round(own, their) for own, their in zip(grad_terms, partner))
    start_row = copy_index * shard_width
    grads = [lax.dynamic_slice_in_dim(each, start_row, shard_width, 0) for each in grad_terms]
    return (output, *grads)


def solution(mesh):
    split = P("expert", "dp")
    pairs = P("expert", None)
    return jax.shard_map(
        per_device,
        mesh=mesh,
        in_specs=(split, pairs, pairs, split, split, split, split),
        out_specs=(split, split, split, split),
        check_vma=False,
    )
```

```python
import jax
import jax.numpy as jnp
from jax import lax
from jax.experimental import pallas as pl
from jax.experimental.pallas import tpu as pltpu
from jax.sharding import PartitionSpec as P

BF = jnp.bfloat16
F32 = jnp.float32


def as_sent(array):

    def short(part):
        return part.astype(BF) if part.dtype == F32 else part

    return jax.tree.map(short, array)


def from_partner(block, axis, bit):
    count = lax.axis_size(axis)
    route = []
    for low in range(count):
        high = low | 1 << bit
        if high != low and high < count:
            route += [(low, high), (high, low)]
    return lax.ppermute(block, axis, route)


def swap(block, axis, mask):
    count = lax.axis_size(axis)
    return lax.ppermute(block, axis, [(i, i ^ mask) for i in range(count)])


def after(values):
    return lax.optimization_barrier(values)


def after_start(value, earlier):
    value, column = after((value, earlier))
    return value, 0.0 * column.astype(F32)


def silu_parts(gate_sum):
    gate_sigmoid = jax.nn.sigmoid(gate_sum)
    return (gate_sum * gate_sigmoid, gate_sigmoid * (1.0 + gate_sum * (1.0 - gate_sigmoid)))


def relay_join(own_part, their_part, is_upper, join_axis):
    lower_first = jnp.concatenate([own_part, their_part], axis=join_axis)
    upper_first = jnp.concatenate([their_part, own_part], axis=join_axis)
    return jnp.where(is_upper, upper_first, lower_first)


def add_round(own_part, their_part):
    return (own_part.astype(F32) + their_part.astype(F32)).astype(BF)


def reorder(rows, key, parts):
    blocks = rows.reshape(parts, rows.shape[0] // parts, rows.shape[1])
    return jnp.concatenate(
        [lax.dynamic_index_in_dim(blocks, key ^ i, 0, keepdims=False) for i in range(parts)], axis=0
    )


def all_to_all(rows, experts):
    moved = lax.all_to_all(
        rows.reshape(experts, rows.shape[0] // experts, rows.shape[1]),
        "expert",
        split_axis=0,
        concat_axis=0,
        tiled=True,
    )
    return moved.reshape(rows.shape)


def pair_core(rows):
    n = rows.shape[0] // 2
    return rows[:n], swap(rows[n:], "expert", 1)


def to_chips(own, other):
    n = own.shape[0] // 4
    blocks = [
        jnp.concatenate([own[m * n:(m + 1) * n], other[m * n:(m + 1) * n]], axis=0) for m in range(4)
    ]
    return [blocks[0]] + [swap(blocks[m], "expert", 2 * m) for m in range(1, 4)]


def to_chips_first(rows):
    n = rows.shape[0] // 8
    blocks = [
        jnp.concatenate([rows[m * n:(m + 1) * n], rows[(4 + m) * n:(5 + m) * n]], axis=0) for m in range(4)
    ]
    return [blocks[0]] + [swap(blocks[m], "expert", 2 * m) for m in range(1, 4)]


def core_last(got):
    n = got[0].shape[0] // 2
    other = swap(jnp.concatenate([each[n:] for each in got], axis=0), "expert", 1)
    rows = []
    for m, each in enumerate(got):
        rows += [each[:n], other[m * n:(m + 1) * n]]
    return rows


def from_chips(rows):
    n = rows.shape[0] // 4
    return [rows[:n]] + [swap(rows[m * n:(m + 1) * n], "expert", 2 * m) for m in range(1, 4)]


def from_core(back):
    n = back[0].shape[0] // 2
    other = swap(jnp.concatenate([each[n:] for each in back], axis=0), "expert", 1)
    return jnp.concatenate([each[:n] for each in back] + [other], axis=0)


def scatter_far(first, second):
    n = first.shape[0] // 4
    return swap(first[3 * n:], "dp", 1), swap(second[3 * n:], "dp", 2)


def scatter_add(first, second, via_x, via_y):
    n = first.shape[0] // 4
    to_x = jnp.concatenate([first[n:2 * n], add_round(second[n:2 * n], via_y)], axis=1)
    to_y = jnp.concatenate([add_round(first[2 * n:3 * n], via_x), second[2 * n:3 * n]], axis=1)
    return to_x, to_y


def scatter_near(first, second, to_x, to_y):
    n = first.shape[0] // 4
    c = first.shape[1]
    from_x = swap(to_x, "dp", 1)
    from_y = swap(to_y, "dp", 2)
    return tuple(
        own[:n].astype(F32) + x.astype(F32) + y.astype(F32)
        for own, x, y in ((first, from_x[:, :c], from_y[:, :c]), (second, from_x[:, c:], from_y[:, c:]))
    )


def gather_near(first, second):
    own = jnp.concatenate([first, second], axis=1)
    return swap(own, "dp", 1), swap(own, "dp", 2)


def gather_far(first, second, from_x, from_y):
    c = first.shape[1]
    far_first = swap(from_y[:, :c], "dp", 1)
    far_second = swap(from_x[:, c:], "dp", 2)
    return (
        jnp.concatenate([first, from_x[:, :c], from_y[:, :c], far_first], axis=0),
        jnp.concatenate([second, from_x[:, c:], from_y[:, c:], far_second], axis=0),
    )


CONTRACT_FEATS = (((1,), (1,)), ((), ()))
CONTRACT_ROWS = (((0,), (0,)), ((), ()))


def two_terms(first, second, rows):
    count, width = first.shape
    feats = rows.shape[1]
    cuts = ((0, width // 2, width), (0, width // 2, width - 256, width))

    def kernel(first_ref, second_ref, rows_ref, first_out, second_out, first_held, second_held, sems):
        copies = []
        refs = ((first_ref, first_out, first_held), (second_ref, second_out, second_held))
        for (left_ref, out, held), ends in zip(refs, cuts):
            for low, high in zip(ends, ends[1:]):
                held[low:high, :] = lax.dot_general(
                    left_ref[:, low:high], rows_ref[...], CONTRACT_ROWS, preferred_element_type=F32
                ).astype(BF)
                copy = pltpu.make_async_copy(held.at[low:high], out.at[low:high], sems.at[len(copies)])
                copy.start()
                copies.append(copy)
        for copy in copies:
            copy.wait()

    whole = pl.BlockSpec(memory_space=pltpu.VMEM)
    anywhere = pl.BlockSpec(memory_space=pl.ANY)
    out = jax.ShapeDtypeStruct((width, feats), BF)
    return pl.pallas_call(
        kernel,
        in_specs=[whole, whole, whole],
        out_specs=[anywhere, anywhere],
        out_shape=[out, out],
        scratch_shapes=[
            pltpu.VMEM((width, feats), BF),
            pltpu.VMEM((width, feats), BF),
            pltpu.SemaphoreType.DMA((5,)),
        ],
        compiler_params=pltpu.CompilerParams(vmem_limit_bytes=36 * 2**20),
        cost_estimate=pl.CostEstimate(
            flops=16 * count * width * feats,
            bytes_accessed=16 * (count + feats) * width,
            transcendentals=0,
        ),
    )(first, second, rows)


def per_device(tokens, expert_ids, route_weights, w_gate, w_up, w_down, out_grad):
    experts = lax.axis_size("expert")
    copies = experts // 8
    levels = copies.bit_length() - 1
    owner_index = lax.axis_index("expert")
    me = lax.axis_index("dp")
    copy_index = owner_index % copies
    tok_rows = tokens.shape[0]
    shard_width = w_gate.shape[0]
    capacity = max(2, 5 * tok_rows // (2 * experts))
    buckets = experts * capacity
    near = experts <= 8
    keys = expert_ids
    if near:
        keys = expert_ids ^ owner_index
        keys = (keys & 1) * 4 + (keys >> 1)

    lanes = jnp.arange(experts, dtype=jnp.int32)[None, :]
    first = keys[:, :1] == lanes
    second = keys[:, 1:] == lanes
    named = (first | second).astype(BF)
    earlier = (
        jnp.arange(tok_rows, dtype=jnp.int32)[None, :] < jnp.arange(tok_rows, dtype=jnp.int32)[:, None]
    ).astype(BF)
    before = jnp.dot(earlier, named, preferred_element_type=F32)
    slots = jnp.arange(buckets, dtype=jnp.int32)[None, :]

    def place(chosen, key):
        rank = jnp.sum(jnp.where(chosen, before, 0.0), axis=1, keepdims=True).astype(jnp.int32)
        return (slots == key * capacity + rank).astype(BF)

    place_0 = place(first, keys[:, :1])
    place_1 = place(second, keys[:, 1:])
    send_rows = lax.dot_general(
        place_0 + place_1, tokens, CONTRACT_ROWS, preferred_element_type=F32
    ).astype(BF)
    grad_f32 = out_grad.astype(F32)
    cot_0 = (route_weights[:, :1] * grad_f32).astype(BF)
    cot_1 = (route_weights[:, 1:] * grad_f32).astype(BF)
    cot_send = (
        lax.dot_general(place_0, cot_0, CONTRACT_ROWS, preferred_element_type=F32)
        + lax.dot_general(place_1, cot_1, CONTRACT_ROWS, preferred_element_type=F32)
    ).astype(BF)
    if near:
        in_rows = to_chips(*pair_core(send_rows))
        cot_send, in_rows[2] = after((cot_send, in_rows[2]))
        cot_rows = to_chips_first(cot_send)
    else:
        in_rows = [all_to_all(send_rows, experts)]
        cot_rows = [all_to_all(cot_send, experts)]
    in_rows = reorder(jnp.concatenate(in_rows, axis=0), me, 4)

    pieces = (w_gate, w_up, w_down)
    for bit_index in range(levels):
        partner = from_partner(as_sent(pieces), "expert", bit_index)
        is_upper = owner_index // 2**bit_index % 2 == 1
        pieces = tuple(relay_join(own, their, is_upper, 0) for own, their in zip(pieces, partner))
    gate_w, up_w, down_w = pieces

    def partial_product(rows, weights):
        return lax.dot_general(rows, weights, CONTRACT_FEATS, preferred_element_type=F32).astype(BF)

    half = gate_w.shape[0] // 2
    part_gate, part_up = partial_product(in_rows, gate_w), partial_product(in_rows, up_w)
    to_x, to_y = scatter_add(part_gate, part_up, *scatter_far(part_gate, part_up))
    gate_sum, up_sum = scatter_near(part_gate, part_up, to_x, to_y)
    cot_rows, zeros = after_start(cot_rows, to_x[:, -1:] + to_y[:, :1])
    if near:
        cot_rows = core_last(cot_rows)
    cot_rows = reorder(jnp.concatenate(cot_rows, axis=0), me, 4)

    active, slope_term = silu_parts(gate_sum)
    own_hidden = (active * up_sum).astype(BF)

    part_hidden = partial_product(cot_rows, down_w)
    part_first, part_second = part_hidden[:, :half], part_hidden[:, half:]
    via, more_zeros = after_start(scatter_far(part_first, part_second), own_hidden[:, :1])
    to_x, to_y = scatter_add(part_first, part_second, *via)
    own_hidden = (own_hidden[:, :half], own_hidden[:, half:])
    near_hidden = gather_near(*own_hidden)
    hidden = jnp.concatenate(gather_far(*own_hidden, *near_hidden), axis=1)
    grad_hidden = jnp.concatenate(scatter_near(part_first, part_second, to_x, to_y), axis=1) + zeros + more_zeros
    out_rows = jnp.dot(hidden, down_w, preferred_element_type=F32).astype(BF)

    own_grads = ((grad_hidden * up_sum * slope_term).astype(BF), (grad_hidden * active).astype(BF))
    hidden, near_grads = after((hidden, gather_near(*own_grads)))
    grad_rows = gather_far(*own_grads, *near_grads)
    back = reorder(out_rows, me, 4)
    if near:
        back, grad_rows = after((from_chips(back), grad_rows))
        returned = from_core(back)
    else:
        returned = all_to_all(back, experts)
    weighted = (route_weights[:, :1] * place_0 + route_weights[:, 1:] * place_1).astype(BF)
    output = jnp.dot(weighted, returned, preferred_element_type=F32).astype(BF)

    def term(left, right):
        return lax.dot_general(left, right, CONTRACT_ROWS, preferred_element_type=F32).astype(BF)

    down_term, grad_rows = after((term(hidden, cot_rows), grad_rows))
    grad_terms = (*two_terms(*grad_rows, in_rows), down_term)
    for bit_index in range(levels):
        partner = from_partner(grad_terms, "expert", bit_index)
        grad_terms = tuple(add_round(own, their) for own, their in zip(grad_terms, partner))
    start_row = copy_index * shard_width
    grads = [lax.dynamic_slice_in_dim(each, start_row, shard_width, 0) for each in grad_terms]
    return (output, *grads)


def solution(mesh):
    split = P("expert", "dp")
    pairs = P("expert", None)
    return jax.shard_map(
        per_device,
        mesh=mesh,
        in_specs=(split, pairs, pairs, split, split, split, split),
        out_specs=(split, split, split, split),
        check_vma=False,
    )
```

```python
import jax
import jax.numpy as jnp
from jax import lax
from jax.experimental import pallas as pl
from jax.experimental.pallas import tpu as pltpu
from jax.sharding import PartitionSpec as P

BF = jnp.bfloat16
F32 = jnp.float32


def as_sent(array):

    def short(part):
        return part.astype(BF) if part.dtype == F32 else part

    return jax.tree.map(short, array)


def from_partner(block, axis, bit):
    count = lax.axis_size(axis)
    route = []
    for low in range(count):
        high = low | 1 << bit
        if high != low and high < count:
            route += [(low, high), (high, low)]
    return lax.ppermute(block, axis, route)


def swap(block, axis, mask):
    count = lax.axis_size(axis)
    return lax.ppermute(block, axis, [(i, i ^ mask) for i in range(count)])


def after(values):
    return lax.optimization_barrier(values)


def after_start(value, earlier):
    value, column = after((value, earlier))
    return value, 0.0 * column.astype(F32)


def silu_parts(gate_sum):
    gate_sigmoid = jax.nn.sigmoid(gate_sum)
    return (gate_sum * gate_sigmoid, gate_sigmoid * (1.0 + gate_sum * (1.0 - gate_sigmoid)))


def relay_join(own_part, their_part, is_upper, join_axis):
    lower_first = jnp.concatenate([own_part, their_part], axis=join_axis)
    upper_first = jnp.concatenate([their_part, own_part], axis=join_axis)
    return jnp.where(is_upper, upper_first, lower_first)


def add_round(own_part, their_part):
    return (own_part.astype(F32) + their_part.astype(F32)).astype(BF)


def reorder(rows, key, parts):
    blocks = rows.reshape(parts, rows.shape[0] // parts, rows.shape[1])
    return jnp.concatenate(
        [lax.dynamic_index_in_dim(blocks, key ^ i, 0, keepdims=False) for i in range(parts)], axis=0
    )


def all_to_all(rows, experts):
    moved = lax.all_to_all(
        rows.reshape(experts, rows.shape[0] // experts, rows.shape[1]),
        "expert",
        split_axis=0,
        concat_axis=0,
        tiled=True,
    )
    return moved.reshape(rows.shape)


def pair_core(rows):
    n = rows.shape[0] // 2
    return rows[:n], swap(rows[n:], "expert", 1)


def to_chips(own, other):
    n = own.shape[0] // 4
    blocks = [
        jnp.concatenate([own[m * n:(m + 1) * n], other[m * n:(m + 1) * n]], axis=0) for m in range(4)
    ]
    return [blocks[0]] + [swap(blocks[m], "expert", 2 * m) for m in range(1, 4)]


def to_chips_first(rows):
    n = rows.shape[0] // 8
    blocks = [
        jnp.concatenate([rows[m * n:(m + 1) * n], rows[(4 + m) * n:(5 + m) * n]], axis=0) for m in range(4)
    ]
    return [blocks[0]] + [swap(blocks[m], "expert", 2 * m) for m in range(1, 4)]


def core_last(got):
    n = got[0].shape[0] // 2
    other = swap(jnp.concatenate([each[n:] for each in got], axis=0), "expert", 1)
    rows = []
    for m, each in enumerate(got):
        rows += [each[:n], other[m * n:(m + 1) * n]]
    return rows


def from_chips(rows):
    n = rows.shape[0] // 4
    return [rows[:n]] + [swap(rows[m * n:(m + 1) * n], "expert", 2 * m) for m in range(1, 4)]


def from_core(back):
    n = back[0].shape[0] // 2
    other = swap(jnp.concatenate([each[n:] for each in back], axis=0), "expert", 1)
    return jnp.concatenate([each[:n] for each in back] + [other], axis=0)


def scatter_far(first, second):
    n = first.shape[0] // 4
    return swap(first[3 * n:], "dp", 1), swap(second[3 * n:], "dp", 2)


def scatter_add(first, second, via_x, via_y):
    n = first.shape[0] // 4
    to_x = jnp.concatenate([first[n:2 * n], add_round(second[n:2 * n], via_y)], axis=1)
    to_y = jnp.concatenate([add_round(first[2 * n:3 * n], via_x), second[2 * n:3 * n]], axis=1)
    return to_x, to_y


def scatter_near(first, second, to_x, to_y):
    n = first.shape[0] // 4
    c = first.shape[1]
    from_x = swap(to_x, "dp", 1)
    from_y = swap(to_y, "dp", 2)
    return tuple(
        own[:n].astype(F32) + x.astype(F32) + y.astype(F32)
        for own, x, y in ((first, from_x[:, :c], from_y[:, :c]), (second, from_x[:, c:], from_y[:, c:]))
    )


def gather_near(first, second):
    own = jnp.concatenate([first, second], axis=1)
    return swap(own, "dp", 1), swap(own, "dp", 2)


def gather_far(first, second, from_x, from_y):
    c = first.shape[1]
    far_first = swap(from_y[:, :c], "dp", 1)
    far_second = swap(from_x[:, c:], "dp", 2)
    return (
        jnp.concatenate([first, from_x[:, :c], from_y[:, :c], far_first], axis=0),
        jnp.concatenate([second, from_x[:, c:], from_y[:, c:], far_second], axis=0),
    )


CONTRACT_FEATS = (((1,), (1,)), ((), ()))
CONTRACT_ROWS = (((0,), (0,)), ((), ()))


def two_terms(first, second, rows):
    count, width = first.shape
    feats = rows.shape[1]
    cuts = ((0, width // 2, width), (0, width // 2, width - 256, width))

    def kernel(first_ref, second_ref, rows_ref, first_out, second_out, first_held, second_held, sems):
        copies = []
        refs = ((first_ref, first_out, first_held), (second_ref, second_out, second_held))
        for (left_ref, out, held), ends in zip(refs, cuts):
            for low, high in zip(ends, ends[1:]):
                held[low:high, :] = lax.dot_general(
                    left_ref[:, low:high], rows_ref[...], CONTRACT_ROWS, preferred_element_type=F32
                ).astype(BF)
                copy = pltpu.make_async_copy(held.at[low:high], out.at[low:high], sems.at[len(copies)])
                copy.start()
                copies.append(copy)
        for copy in copies:
            copy.wait()

    whole = pl.BlockSpec(memory_space=pltpu.VMEM)
    anywhere = pl.BlockSpec(memory_space=pl.ANY)
    out = jax.ShapeDtypeStruct((width, feats), BF)
    return pl.pallas_call(
        kernel,
        in_specs=[whole, whole, whole],
        out_specs=[anywhere, anywhere],
        out_shape=[out, out],
        scratch_shapes=[
            pltpu.VMEM((width, feats), BF),
            pltpu.VMEM((width, feats), BF),
            pltpu.SemaphoreType.DMA((5,)),
        ],
        compiler_params=pltpu.CompilerParams(vmem_limit_bytes=36 * 2**20),
        cost_estimate=pl.CostEstimate(
            flops=16 * count * width * feats,
            bytes_accessed=16 * (count + feats) * width,
            transcendentals=0,
        ),
    )(first, second, rows)


def per_device(tokens, expert_ids, route_weights, w_gate, w_up, w_down, out_grad):
    experts = lax.axis_size("expert")
    copies = experts // 8
    levels = copies.bit_length() - 1
    owner_index = lax.axis_index("expert")
    me = lax.axis_index("dp")
    copy_index = owner_index % copies
    tok_rows = tokens.shape[0]
    shard_width = w_gate.shape[0]
    capacity = max(2, 5 * tok_rows // (2 * experts))
    buckets = experts * capacity
    near = experts <= 8
    keys = expert_ids
    if near:
        keys = expert_ids ^ owner_index
        keys = (keys & 1) * 4 + (keys >> 1)

    lanes = jnp.arange(experts, dtype=jnp.int32)[None, :]
    first = keys[:, :1] == lanes
    second = keys[:, 1:] == lanes
    named = (first | second).astype(BF)
    earlier = (
        jnp.arange(tok_rows, dtype=jnp.int32)[None, :] < jnp.arange(tok_rows, dtype=jnp.int32)[:, None]
    ).astype(BF)
    before = jnp.dot(earlier, named, preferred_element_type=F32)
    slots = jnp.arange(buckets, dtype=jnp.int32)[None, :]

    def place(chosen, key):
        rank = jnp.sum(jnp.where(chosen, before, 0.0), axis=1, keepdims=True).astype(jnp.int32)
        return (slots == key * capacity + rank).astype(BF)

    place_0 = place(first, keys[:, :1])
    place_1 = place(second, keys[:, 1:])
    send_rows = lax.dot_general(
        place_0 + place_1, tokens, CONTRACT_ROWS, preferred_element_type=F32
    ).astype(BF)
    grad_f32 = out_grad.astype(F32)
    cot_0 = (route_weights[:, :1] * grad_f32).astype(BF)
    cot_1 = (route_weights[:, 1:] * grad_f32).astype(BF)
    cot_send = (
        lax.dot_general(place_0, cot_0, CONTRACT_ROWS, preferred_element_type=F32)
        + lax.dot_general(place_1, cot_1, CONTRACT_ROWS, preferred_element_type=F32)
    ).astype(BF)
    if near:
        in_rows = to_chips(*pair_core(send_rows))
        cot_send, in_rows[1] = after((cot_send, in_rows[1]))
        cot_rows = to_chips_first(cot_send)
    else:
        in_rows = [all_to_all(send_rows, experts)]
        cot_rows = [all_to_all(cot_send, experts)]
    in_rows = reorder(jnp.concatenate(in_rows, axis=0), me, 4)

    pieces = (w_gate, w_up, w_down)
    for bit_index in range(levels):
        partner = from_partner(as_sent(pieces), "expert", bit_index)
        is_upper = owner_index // 2**bit_index % 2 == 1
        pieces = tuple(relay_join(own, their, is_upper, 0) for own, their in zip(pieces, partner))
    gate_w, up_w, down_w = pieces

    def partial_product(rows, weights):
        return lax.dot_general(rows, weights, CONTRACT_FEATS, preferred_element_type=F32).astype(BF)

    half = gate_w.shape[0] // 2
    part_gate, part_up = partial_product(in_rows, gate_w), partial_product(in_rows, up_w)
    to_x, to_y = scatter_add(part_gate, part_up, *scatter_far(part_gate, part_up))
    gate_sum, up_sum = scatter_near(part_gate, part_up, to_x, to_y)
    cot_rows, zeros = after_start(cot_rows, to_x[:, -1:] + to_y[:, :1])
    if near:
        cot_rows = core_last(cot_rows)
    cot_rows = reorder(jnp.concatenate(cot_rows, axis=0), me, 4)

    active, slope_term = silu_parts(gate_sum)
    own_hidden = (active * up_sum).astype(BF)

    part_hidden = partial_product(cot_rows, down_w)
    part_first, part_second = part_hidden[:, :half], part_hidden[:, half:]
    via, more_zeros = after_start(scatter_far(part_first, part_second), own_hidden[:, :1])
    to_x, to_y = scatter_add(part_first, part_second, *via)
    own_hidden = (own_hidden[:, :half], own_hidden[:, half:])
    near_hidden = gather_near(*own_hidden)
    hidden = jnp.concatenate(gather_far(*own_hidden, *near_hidden), axis=1)
    grad_hidden = jnp.concatenate(scatter_near(part_first, part_second, to_x, to_y), axis=1) + zeros + more_zeros
    out_rows = jnp.dot(hidden, down_w, preferred_element_type=F32).astype(BF)

    own_grads = ((grad_hidden * up_sum * slope_term).astype(BF), (grad_hidden * active).astype(BF))
    hidden, near_grads = after((hidden, gather_near(*own_grads)))
    grad_rows = gather_far(*own_grads, *near_grads)
    back = reorder(out_rows, me, 4)
    if near:
        back, grad_rows = after((from_chips(back), grad_rows))
        returned = from_core(back)
    else:
        returned = all_to_all(back, experts)
    weighted = (route_weights[:, :1] * place_0 + route_weights[:, 1:] * place_1).astype(BF)
    output = jnp.dot(weighted, returned, preferred_element_type=F32).astype(BF)

    def term(left, right):
        return lax.dot_general(left, right, CONTRACT_ROWS, preferred_element_type=F32).astype(BF)

    down_term, grad_rows = after((term(hidden, cot_rows), grad_rows))
    grad_terms = (*two_terms(*grad_rows, in_rows), down_term)
    for bit_index in range(levels):
        partner = from_partner(grad_terms, "expert", bit_index)
        grad_terms = tuple(add_round(own, their) for own, their in zip(grad_terms, partner))
    start_row = copy_index * shard_width
    grads = [lax.dynamic_slice_in_dim(each, start_row, shard_width, 0) for each in grad_terms]
    return (output, *grads)


def solution(mesh):
    split = P("expert", "dp")
    pairs = P("expert", None)
    return jax.shard_map(
        per_device,
        mesh=mesh,
        in_specs=(split, pairs, pairs, split, split, split, split),
        out_specs=(split, split, split, split),
        check_vma=False,
    )
```
